32 devices in a mesh: seq: 4 (over y, x), mp: 8 (over z, core).
Axes of the slice: x: 2, y: 2, z: 4, core: 2. Of those that a mesh axis runs over, the one named last changes fastest.
Arguments:
- x_in: bfloat16 [4096, 8192], P('seq', 'mp'), may hold values from -6 to 6
- step_size: bfloat16 [4096, 128], P('seq', 'mp'), may hold values from 0.5 to 1.5
- log_keep: bfloat16 [4096, 128], P('seq', 'mp'), may hold values from -0.6 to 0, as said below
- b_proj: bfloat16 [4096, 128], P(('seq', 'mp')), may hold values from -0.03125 to 0.03125
- c_proj: bfloat16 [4096, 128], P(('seq', 'mp')), may hold values from -6 to 6
- y_grad: bfloat16 [4096, 8192], P('seq', 'mp'), may hold values from -6 to 6
- layer_input: bfloat16 [4096, 4096], P('seq', 'mp'), may hold values from -30 to 30
Outputs:
- y_out: bfloat16 [4096, 8192], P('seq', 'mp')
- x_grad: bfloat16 [4096, 8192], P('seq', 'mp')
- in_factor: float32 [512, 4096], P('seq', 'mp')
- grad_factor: float32 [1024, 8192], P('seq', 'mp')
The draws below stay inside these ranges and needn't reach their ends.
Inputs may be any that keep to these rules, and one draw needn't show every extreme that they name: `log_keep`: negative in every entry.
All inputs are finite; a program needn't handle non-finite values.
Results may differ from the reference program's by a relative error of at most 0.017.
Values may be sent and summed in bfloat16 or wider, within the bound.
No kernel may reach another device: no remote copies, remote signals or barrier semaphores. Data moves between devices by JAX's collectives and lax.ppermute only.
A program may use at most 128 MiB of HBM per device.

```python
import jax
import jax.numpy as jnp
from jax import lax

D = 4096
HEADS = 128
HEAD_DIM = 64
STATE = 128
SPAN = 256
TOK_DEV = 1024
STEP_TOTAL = 4096
BLOCK_IN = 512
BLOCK_OUT = 1024


def draw_log_keep(key, part):
    stochastic_seed_list = jax.random.split(key, 7)
    fraction = 0.5
    is_fast = jax.random.uniform(stochastic_seed_list[0], (HEADS,)) < fraction
    fast_rate = jax.random.uniform(stochastic_seed_list[1], (HEADS,), minval=1.0 / 50.0, maxval=1.0 / 30.0)
    slow_rate = jax.random.uniform(stochastic_seed_list[2], (HEADS,), minval=0.2, maxval=0.6) / STEP_TOTAL
    decay_rate = jnp.where(is_fast, fast_rate, slow_rate)
    block_total = STEP_TOTAL // TOK_DEV
    spread = jnp.exp(jax.random.uniform(stochastic_seed_list[3], (block_total, HEADS), minval=-0.7, maxval=0.7))
    spread = jnp.repeat(spread, TOK_DEV, axis=0)
    roughness = jax.random.uniform(stochastic_seed_list[4], (STEP_TOTAL, HEADS), minval=0.5, maxval=1.5)
    reference_result = -decay_rate[None, :] * spread * roughness
    location_offsets = jax.random.randint(stochastic_seed_list[5], (3,), 0, STEP_TOTAL)
    segment_step_selector = jnp.any(jnp.arange(STEP_TOTAL)[:, None] == location_offsets[None, :], axis=1)
    segment_retain_choice = jnp.log(jax.random.uniform(stochastic_seed_list[6], (STEP_TOTAL, 1), minval=0.6, maxval=0.8))
    return jnp.where(segment_step_selector[:, None], segment_retain_choice, reference_result).astype(jnp.bfloat16)


def draw_layer_input(key, part):
    stochastic_seed_list = jax.random.split(key, 3)
    ramp = jnp.sqrt(1.0 + 2.0 * jnp.arange(STEP_TOTAL, dtype=jnp.float32) / STEP_TOTAL)
    row_scale = jnp.exp(jax.random.uniform(stochastic_seed_list[0], (STEP_TOTAL, 1), minval=-0.6931, maxval=0.6931)) * ramp[:, None]
    column_scale = jnp.exp(jax.random.uniform(stochastic_seed_list[1], (1, D), minval=-0.6931, maxval=0.6931))
    entries = jnp.clip(jax.random.normal(stochastic_seed_list[2], (STEP_TOTAL, D)), -4.0, 4.0)
    return (entries * row_scale * column_scale).astype(jnp.bfloat16)


def steps_of(rng, dims, shards, low, top_value):
    factor_of = 1.0
    for axis_at, shards_of in shards:
        steps = jax.random.uniform(jax.random.fold_in(jax.random.fold_in(rng, 6), axis_at), (shards_of,), jnp.float32, low / len(shards), top_value / len(shards))
        factor_of = factor_of * jnp.repeat(jnp.exp(steps), dims[axis_at] // shards_of).reshape((-1,) + (1,) * (len(dims) - 1 - axis_at))
    return factor_of


def bell_draw(own_key, extent, scale, bound, cuts=(), kind=jnp.bfloat16):
    values = scale * jax.random.normal(own_key, extent, jnp.float32)
    if cuts:
        values = values * steps_of(own_key, extent, cuts, -0.22, 0.18)
    return jnp.clip(values, -bound, bound).astype(kind)


def setup_inputs(seed: int = 0) -> dict:
    keys = jax.random.split(jax.random.key(seed), 8)
    return {
        "x_in": bell_draw(keys[0], (STEP_TOTAL, HEADS * HEAD_DIM), 1.0, 6.0, ((0, 4), (1, 8))),
        "step_size": jnp.clip(0.5 + 1.0 * jax.random.uniform(keys[1], (STEP_TOTAL, HEADS), jnp.float32) ** steps_of(keys[1], (STEP_TOTAL, HEADS), ((0, 4), (1, 8)), -0.2, 0.2), 0.5, 1.5).astype(jnp.bfloat16),
        "log_keep": draw_log_keep(jax.random.fold_in(keys[7], 71), 0),
        "b_proj": bell_draw(keys[3], (STEP_TOTAL, STATE), (4 * (STATE * STEP_TOTAL) ** -0.5), 0.03125, ((0, 32),)),
        "c_proj": bell_draw(keys[4], (STEP_TOTAL, STATE), 1.0, 6.0, ((0, 32),)),
        "y_grad": bell_draw(keys[5], (STEP_TOTAL, HEADS * HEAD_DIM), 1.0, 6.0, ((0, 4), (1, 8))),
        "layer_input": draw_layer_input(jax.random.fold_in(keys[7], 71), 0),
    }


def merge_pair(earlier, later):
    return (earlier[0] * later[0], later[0][..., None, None] * earlier[1] + later[1])


def as_float(array):
    return array.astype(jnp.float32)


def rounded(array):
    return as_float(lax.optimization_barrier(array.astype(jnp.bfloat16)))


def ssd_pass(values, step_vals, keep_logs, b_rows, c_rows, grad_vals):
    sequence_length, head_count, channels = values.shape
    block_count = sequence_length // SPAN
    val_blocks = as_float(values).reshape(block_count, SPAN, head_count, channels)
    grad_blocks = as_float(grad_vals).reshape(block_count, SPAN, head_count, channels)
    step_blocks = as_float(step_vals).reshape(block_count, SPAN, head_count)
    running = jnp.cumsum(as_float(keep_logs).reshape(block_count, SPAN, head_count), axis=1)
    b_blocks = as_float(b_rows).reshape(block_count, SPAN, -1)
    c_blocks = as_float(c_rows).reshape(block_count, SPAN, -1)
    score = jnp.einsum('cin,cjn->cij', c_blocks, b_blocks)
    running_t = jnp.swapaxes(running, 1, 2)
    lower = jnp.arange(SPAN)[:, None] >= jnp.arange(SPAN)[None, :]
    decay = jnp.exp(jnp.where(lower, running_t[:, :, :, None] - running_t[:, :, None, :], -jnp.inf))
    weight = rounded(decay * score[:, None] * jnp.swapaxes(step_blocks, 1, 2)[:, :, None, :])
    inner_out = jnp.einsum('chij,cjhp->cihp', weight, val_blocks)
    inner_grad = jnp.einsum('chij,cihp->cjhp', weight, grad_blocks)
    final_log = running[:, -1:, :]
    tail_scale = step_blocks * jnp.exp(final_log - running)
    lead_scale = jnp.exp(running)
    block_state = jnp.einsum('cjhp,cjn->chpn', rounded(val_blocks * tail_scale[..., None]), b_blocks)
    block_back = jnp.einsum('cihp,cin->chpn', rounded(grad_blocks * lead_scale[..., None]), c_blocks)
    block_decay = jnp.exp(final_log[:, 0, :])
    fwd_decay, fwd_state = lax.associative_scan(merge_pair, (block_decay, block_state), axis=0)
    rev_decay, rev_state = lax.associative_scan(merge_pair, (block_decay, block_back), axis=0, reverse=True)
    zero_state = jnp.zeros_like(block_state[0])
    start_state = jnp.concatenate([zero_state[None], fwd_state[:-1]], axis=0)
    back_state = jnp.concatenate([rev_state[1:], zero_state[None]], axis=0)
    y_blocks = inner_out + lead_scale[..., None] * jnp.einsum('cin,chpn->cihp', c_blocks, rounded(start_state))
    dx_blocks = inner_grad + tail_scale[..., None] * jnp.einsum('cjn,chpn->cjhp', b_blocks, rounded(back_state))
    out_vals = y_blocks.astype(jnp.bfloat16).reshape(sequence_length, head_count, channels)
    grad_out = dx_blocks.astype(jnp.bfloat16).reshape(sequence_length, head_count, channels)
    return out_vals, grad_out


def block_gram(matrix, block_width):
    results = []
    for column_block in range(matrix.shape[1] // block_width):
        part_cols = matrix[:, column_block * block_width:(column_block + 1) * block_width]
        results.append(jnp.dot(part_cols.T, part_cols, preferred_element_type=jnp.float32) / STEP_TOTAL)
    return jnp.concatenate(results, axis=1)


def reference(x_in, step_size, log_keep, b_proj, c_proj, y_grad, layer_input):
    sequence_length = x_in.shape[0]

    def head_major(array):
        return array.reshape(sequence_length, HEADS, HEAD_DIM).transpose(1, 0, 2)

    def one_head(entries):
        values, grad_vals, step_vals, keep_logs = entries
        out_vals, grad_out = ssd_pass(values[:, None, :], step_vals[:, None], keep_logs[:, None], b_proj, c_proj, grad_vals[:, None, :])
        return out_vals[:, 0, :], grad_out[:, 0, :]

    outputs, input_grads = lax.map(one_head, (head_major(x_in), head_major(y_grad), step_size.T, log_keep.T))
    y_out = outputs.transpose(1, 0, 2).reshape(sequence_length, HEADS * HEAD_DIM)
    x_grad = input_grads.transpose(1, 0, 2).reshape(sequence_length, HEADS * HEAD_DIM)
    in_factor = block_gram(layer_input, BLOCK_IN)
    grad_factor = block_gram(x_grad, BLOCK_OUT)
    return (y_out, x_grad, in_factor, grad_factor)
```

```python
import functools

import jax
import jax.numpy as jnp
import numpy as np
from jax import lax
from jax.experimental import pallas as pl
from jax.experimental.pallas import tpu as pltpu
from jax.sharding import PartitionSpec as P

HEAD_DIM = 64
SPAN = 256
F32 = jnp.float32
BF16 = jnp.bfloat16
ROWS = 8
LANES = 128


def iota(shape, axis):
    return lax.broadcasted_iota(jnp.int32, shape, axis)


def params(mib=40):
    return pltpu.CompilerParams(vmem_limit_bytes=mib << 20)


def dot(left, right, left_axis=1, right_axis=0):
    return lax.dot_general(
        left, right, (((left_axis,), (right_axis,)), ((), ())), preferred_element_type=F32
    )


def spread(heads, width, first_group):
    lane = iota((LANES, width), 0)
    group = lane // heads
    hit = (lane % heads == iota((LANES, width), 1) // HEAD_DIM) & (group >= first_group)
    return (hit & (group < first_group + 2)).astype(BF16)


def split_parts(values, is_low):
    high = values.astype(BF16)
    low = (values - high.astype(F32)).astype(BF16)
    return jnp.where(is_low, low.astype(F32), high.astype(F32)).astype(BF16)


def scale_body(x_ref, g_ref, step_ref, keep_ref, xv_ref, gu_ref, packed_ref, decay_ref):
    width = x_ref.shape[1]
    heads = step_ref.shape[1]
    copies = (iota((heads, LANES), 1) % heads == iota((heads, LANES), 0)) & (
        iota((heads, LANES), 1) < 4 * heads
    )
    copies = copies.astype(BF16)
    lower = (iota((SPAN, SPAN), 0) >= iota((SPAN, SPAN), 1)).astype(BF16)
    keep = dot(keep_ref[...], copies).astype(BF16)
    step = dot(step_ref[...], copies)
    cum = dot(lower, keep)
    mid = cum[SPAN // 2 - 1 : SPAN // 2]
    end = cum[SPAN - 1 : SPAN]
    group = iota((SPAN, LANES), 1) // heads
    is_low = group % 2 == 1
    offset = cum - mid
    factor = jnp.exp(jnp.where(group < 2, offset, -offset)) * jnp.where(group < 2, 1.0, step)
    packed = split_parts(factor, is_low)
    packed_ref[...] = packed
    take_u = spread(heads, width, 0)
    take_v = spread(heads, width, 2)
    gu_ref[...] = (g_ref[...].astype(F32) * dot(packed, take_u)).astype(BF16)
    xv_ref[...] = (x_ref[...].astype(F32) * dot(packed, take_v)).astype(BF16)
    row = iota((ROWS, LANES), 0)
    logs = jnp.where(row == 0, mid, jnp.where(row == 1, end - mid, end))
    decay_ref[...] = dot(split_parts(jnp.exp(logs), is_low[:ROWS]), take_u)


def scale_inputs(x_in, y_grad, step_size, log_keep):
    rows, width = x_in.shape
    heads = step_size.shape[1]
    blocks = rows // SPAN
    wide = pl.BlockSpec((SPAN, width), lambda k: (k, 0))
    thin = pl.BlockSpec((SPAN, heads), lambda k: (k, 0))
    return pl.pallas_call(
        scale_body,
        grid=(blocks,),
        in_specs=[wide, wide, thin, thin],
        out_specs=[
            wide,
            wide,
            pl.BlockSpec((SPAN, LANES), lambda k: (k, 0)),
            pl.BlockSpec((ROWS, width), lambda k: (k, 0)),
        ],
        out_shape=[
            jax.ShapeDtypeStruct((rows, width), BF16),
            jax.ShapeDtypeStruct((rows, width), BF16),
            jax.ShapeDtypeStruct((rows, LANES), BF16),
            jax.ShapeDtypeStruct((blocks * ROWS, width), F32),
        ],
        compiler_params=params(),
        name="scale_inputs",
    )(x_in, y_grad, step_size, log_keep)


def state_body(proj_ref, val_ref, decay_ref, own_ref, left_ref, right_ref, carry, *, pick):
    own = dot(proj_ref[...], val_ref[...], 0, 0) * decay_ref[pick : pick + 1]
    own_ref[...] = own

    @pl.when(pl.program_id(0) == 0)
    def _():
        carry[...] = own

    @pl.when(pl.program_id(0) > 0)
    def _():
        carry[...] = carry[...] * decay_ref[2:3] + own

    half = left_ref.shape[1]

    @pl.when(pl.program_id(0) == pl.num_programs(0) - 1)
    def _():
        left_ref[...] = carry[:, :half].astype(BF16)
        right_ref[...] = carry[:, half:].astype(BF16)


def device_state(projections, values, decays, backward):
    rows, width = values.shape
    state = projections.shape[1] // 2
    blocks = rows // SPAN
    at = (lambda k: blocks - 1 - k) if backward else (lambda k: k)
    side = 1 if backward else 0
    half = pl.BlockSpec((state, width // 2), lambda k: (0, 0))
    return pl.pallas_call(
        functools.partial(state_body, pick=0 if backward else 1),
        grid=(blocks,),
        in_specs=[
            pl.BlockSpec((SPAN, state), lambda k: (at(k), side)),
            pl.BlockSpec((SPAN, width), lambda k: (at(k), 0)),
            pl.BlockSpec((ROWS, width), lambda k: (at(k), 0)),
        ],
        out_specs=[pl.BlockSpec((state, width), lambda k: (at(k), 0)), half, half],
        out_shape=[
            jax.ShapeDtypeStruct((blocks * state, width), F32),
            jax.ShapeDtypeStruct((state, width // 2), BF16),
            jax.ShapeDtypeStruct((state, width // 2), BF16),
        ],
        scratch_shapes=[pltpu.VMEM((state, width), F32)],
        compiler_params=params(),
        name="back_state" if backward else "front_state",
    )(projections, values, decays)


def apply_block(proj_ref, val_ref, packed_ref, decay_ref, own_ref, carry, backward):
    state = proj_ref.shape[1] // 2
    width = val_ref.shape[1]
    heads = width // HEAD_DIM
    b_rows = proj_ref[:, :state]
    c_rows = proj_ref[:, state:]
    rows_of, cols_of = (b_rows, c_rows) if backward else (c_rows, b_rows)
    score = dot(rows_of, cols_of, 1, 1)
    down, across = iota((SPAN, SPAN), 0), iota((SPAN, SPAN), 1)
    keep = down <= across if backward else down >= across
    score = jnp.where(keep, score, 0.0).astype(BF16)
    entering = carry[...]
    pick = 1 if backward else 0
    total = dot(score, val_ref[...]) + dot(
        rows_of, (entering * decay_ref[pick : pick + 1]).astype(BF16)
    )
    result = (total * dot(packed_ref[...], spread(heads, width, 2 if backward else 0))).astype(BF16)
    carry[...] = entering * decay_ref[2:3] + own_ref[...]
    return result


def enter(early_refs, late_refs, mix_ref, carry):
    half = carry.shape[1] // 2
    for at in range(2):
        cols = slice(at * half, (at + 1) * half)
        carry[:, cols] = (
            early_refs[at][...].astype(F32) * mix_ref[0:1, cols]
            + late_refs[at][...].astype(F32) * mix_ref[1:2, cols]
        )


def front_body(
    proj_ref, val_ref, packed_ref, decay_ref, own_ref, e0, e1, l0, l1, mix_ref, out_ref, carry
):
    @pl.when(pl.program_id(0) == 0)
    def _():
        enter((e0, e1), (l0, l1), mix_ref, carry)

    out_ref[...] = apply_block(proj_ref, val_ref, packed_ref, decay_ref, own_ref, carry, False)


def back_body(
    seq_ref, proj_ref, val_ref, packed_ref, decay_ref, own_ref, e0, e1, l0, l1, mix_ref, out_ref, *rest
):
    gram_refs, (carry, kept) = rest[:-2], rest[-2:]
    step = pl.program_id(0)
    blocks = pl.num_programs(0)

    @pl.when(step == 0)
    def _():
        enter((e0, e1), (l0, l1), mix_ref, carry)

    result = apply_block(proj_ref, val_ref, packed_ref, decay_ref, own_ref, carry, True)
    out_ref[...] = result
    kept[pl.ds(pl.multiple_of((blocks - 1 - step) * SPAN, SPAN), SPAN), :] = result

    @pl.when(step == blocks - 1)
    def _():
        if len(gram_refs) == 1:
            gram_refs[0][...] = dot(kept[...], kept[...], 0, 0).astype(BF16)
            return
        x3, y3, x1, y2, x0, x2, y0, y1 = gram_refs
        width = kept.shape[1]
        part, half = width // 4, width // 2
        for flip, left, right in ((3, x3, y3), (1, x1, y1), (2, x2, y2), (0, x0, y0)):
            start = pl.multiple_of((seq_ref[0] ^ flip) * part, part)
            gram = dot(kept[:, pl.ds(start, part)], kept[...], 0, 0)
            left[...] = gram[:, :half].astype(BF16)
            right[...] = gram[:, half:].astype(BF16)


def apply_specs(rows, width, state, backward):
    blocks = rows // SPAN
    at = (lambda k: blocks - 1 - k) if backward else (lambda k: k)
    whole = lambda shape: pl.BlockSpec(shape, lambda k, *_: (0, 0))
    half = whole((state, width // 2))
    wide = pl.BlockSpec((SPAN, width), lambda k, *_: (at(k), 0))
    specs = [
        pl.BlockSpec((SPAN, 2 * state), lambda k, *_: (at(k), 0)),
        wide,
        pl.BlockSpec((SPAN, LANES), lambda k, *_: (at(k), 0)),
        pl.BlockSpec((ROWS, width), lambda k, *_: (at(k), 0)),
        pl.BlockSpec((state, width), lambda k, *_: (at(k), 0)),
        half,
        half,
        half,
        half,
        whole((ROWS, width)),
    ]
    return blocks, specs, wide, whole


def front_outputs(projections, values, packed, decays, own, early, late, mix):
    rows, width = values.shape
    state = projections.shape[1] // 2
    blocks, specs, wide, _ = apply_specs(rows, width, state, False)
    return pl.pallas_call(
        front_body,
        grid=(blocks,),
        in_specs=specs,
        out_specs=wide,
        out_shape=jax.ShapeDtypeStruct((rows, width), BF16),
        scratch_shapes=[pltpu.VMEM((state, width), F32)],
        compiler_params=params(),
        name="front_outputs",
    )(projections, values, packed, decays, own, *early, *late, mix)


def back_outputs(seq_at, projections, values, packed, decays, own, early, late, mix, square):
    rows, width = values.shape
    state = projections.shape[1] // 2
    blocks, specs, wide, whole = apply_specs(rows, width, state, True)
    if square:
        gram_shapes = [(width // 4, width // 2)] * 8
    else:
        gram_shapes = [(width, width)]
    return pl.pallas_call(
        back_body,
        grid_spec=pltpu.PrefetchScalarGridSpec(
            num_scalar_prefetch=1,
            grid=(blocks,),
            in_specs=specs,
            out_specs=[wide] + [whole(shape) for shape in gram_shapes],
            scratch_shapes=[pltpu.VMEM((state, width), F32), pltpu.VMEM((rows, width), BF16)],
        ),
        out_shape=[jax.ShapeDtypeStruct((rows, width), BF16)]
        + [jax.ShapeDtypeStruct(shape, BF16) for shape in gram_shapes],
        compiler_params=params(),
        name="back_outputs",
    )(seq_at, projections, values, packed, decays, own, *early, *late, mix)


def gather_rows(rows_in):
    count, width = rows_in.shape
    mp_count = lax.axis_size("mp")
    z_count = mp_count // 2
    z_at = lax.axis_index("mp") // 2
    core = lax.axis_index("mp") % 2
    pieces = [rows_in]
    for shift in range(1, z_count):
        perm = [(m, (m + 2 * shift) % mp_count) for m in range(mp_count)]
        pieces.append(lax.ppermute(rows_in, "mp", perm))
    mine = jnp.stack(pieces)
    other = lax.ppermute(mine, "mp", [(m, m ^ 1) for m in range(mp_count)])
    order = (z_at - jnp.arange(z_count)) % z_count
    first = jnp.where(core == 0, mine, other)
    second = jnp.where(core == 0, other, mine)
    return jnp.stack([first, second], axis=1)[order].reshape(mp_count * count, width)


X_PAIRS = [(0, 1), (1, 0), (2, 3), (3, 2)]
Y_PAIRS = [(0, 2), (2, 0), (1, 3), (3, 1)]


def pair_mix(decay_all, seq_at, width):
    d1, d2 = (jnp.repeat(decay_all[i], HEAD_DIM) for i in (1, 2))
    one, zero = jnp.ones((width,), F32), jnp.zeros((width,), F32)
    left = np.arange(width) < width // 2
    table = [
        (jnp.where(left, zero, zero), jnp.where(left, zero, one), jnp.where(left, one, d1), jnp.where(left, d1, one)),
        (jnp.where(left, zero, one), jnp.where(left, zero, d1 * d2), jnp.where(left, zero, d2), one),
        (jnp.where(left, one, zero), jnp.where(left, d2, zero), jnp.where(left, one, zero), jnp.where(left, zero, one)),
        (jnp.where(left, d2, one), jnp.where(left, one, zero), zero, zero),
    ]
    table = jnp.stack([jnp.stack(row) for row in table])
    return lax.dynamic_index_in_dim(table, seq_at, 0, keepdims=False)


def exchange_square(left, right, mix, mirror):
    half = left.shape[1]
    flip = (lambda pairs: [(3 - a, 3 - b) for a, b in pairs]) if mirror else (lambda pairs: pairs)
    go = lambda value, pairs: lax.ppermute(value, "seq", flip(pairs))
    left_one = go(left, [(1, 0), (3, 2), (2, 3)])
    right_one = go(right, [(2, 0), (3, 1)])
    send = lambda own, got, cols: (own.astype(F32) * mix[0, cols] + got.astype(F32) * mix[1, cols]).astype(BF16)
    left_two = go(send(left, left_one, slice(0, half)), [(2, 0), (3, 1)])
    right_two = go(send(right, right_one, slice(half, None)), [(0, 1), (1, 0), (3, 2)])
    rows = jnp.concatenate([mix[2:4], jnp.zeros((ROWS - 2, mix.shape[1]), F32)])
    return (left_one, right_one), (left_two, right_two), rows


def exchange_any(left, right, decay_all, seq_at, backward):
    seq_count = decay_all.shape[0]
    width = left.shape[1] * 2
    totals = lax.all_gather(jnp.concatenate([left, right], axis=1), "seq")
    if not backward:
        totals, decay_all, seq_at = totals[::-1], decay_all[::-1], seq_count - 1 - seq_at
    entering = jnp.zeros((left.shape[0], width), F32)
    for at in range(seq_count - 1, 0, -1):
        moved = jnp.repeat(decay_all[at], HEAD_DIM) * entering + totals[at].astype(F32)
        entering = jnp.where(at > seq_at, moved, entering)
    high = entering.astype(BF16)
    low = (entering - high.astype(F32)).astype(BF16)
    rows = jnp.concatenate([jnp.ones((2, width), F32), jnp.zeros((ROWS - 2, width), F32)])
    half = width // 2
    return (high[:, :half], high[:, half:]), (low[:, :half], low[:, half:]), rows


def exchange(left, right, decay_all, seq_at, backward, square):
    if not square:
        return exchange_any(left, right, decay_all, seq_at, backward)
    if backward:
        mix = pair_mix(decay_all, seq_at, left.shape[1] * 2)
    else:
        mix = pair_mix(decay_all[::-1], 3 - seq_at, left.shape[1] * 2)
    return exchange_square(left, right, mix, not backward)


def scatter_square(x3, y3, x1, y2, x0, x2, y0, y1):
    go = lambda value, pairs: lax.ppermute(value, "seq", pairs)
    x3_in, y3_in = go(x3, X_PAIRS), go(y3, Y_PAIRS)
    x1_in, y2_in = go(x1, X_PAIRS), go(y2, Y_PAIRS)
    x_two = go((x3_in.astype(F32) + x2.astype(F32)).astype(BF16), Y_PAIRS)
    y_two = go((y3_in.astype(F32) + y1.astype(F32)).astype(BF16), X_PAIRS)
    left = x1_in.astype(F32) + x0.astype(F32) + x_two.astype(F32)
    right = y2_in.astype(F32) + y0.astype(F32) + y_two.astype(F32)
    return jnp.concatenate([left, right], axis=1)


def shards(x_in, step_size, log_keep, b_proj, c_proj, y_grad, layer_input):
    tok_rows = x_in.shape[0]
    seq_count = lax.axis_size("seq")
    seq_at = lax.axis_index("seq")
    square = seq_count == 4
    seq_total = tok_rows * seq_count
    decay_all = lax.all_gather(jnp.exp(jnp.sum(log_keep.astype(F32), axis=0)), "seq")
    projections = gather_rows(jnp.concatenate([b_proj, c_proj], axis=1))
    in_gram = dot(layer_input, layer_input, 0, 0).astype(BF16)
    in_sum = lax.psum_scatter(in_gram, "seq", scatter_dimension=0, tiled=True)
    in_factor = in_sum.astype(F32) / seq_total
    xv, gu, packed, decays = scale_inputs(x_in, y_grad, step_size, log_keep)
    own_back, left_back, right_back = device_state(projections, gu, decays, True)
    back_in = exchange(left_back, right_back, decay_all, seq_at, True, square)
    own_front, left_front, right_front = device_state(projections, xv, decays, False)
    front_in = exchange(left_front, right_front, decay_all, seq_at, False, square)
    x_grad, *grams = back_outputs(
        seq_at.reshape(1).astype(jnp.int32), projections, gu, packed, decays, own_back, *back_in, square
    )
    y_out = front_outputs(projections, xv, packed, decays, own_front, *front_in)
    if square:
        grad_sum = scatter_square(*grams)
    else:
        grad_sum = lax.psum_scatter(grams[0], "seq", scatter_dimension=0, tiled=True).astype(F32)
    return (y_out, x_grad, in_factor, grad_sum / seq_total)


def solution(mesh):
    spec = P("seq", "mp")
    rows = P(("seq", "mp"), None)
    return jax.shard_map(
        shards,
        mesh=mesh,
        in_specs=(spec, spec, spec, rows, rows, spec, spec),
        out_specs=(spec, spec, spec, spec),
        check_vma=False,
    )
```

```python
import functools

import jax
import jax.numpy as jnp
import numpy as np
from jax import lax
from jax.experimental import pallas as pl
from jax.experimental.pallas import tpu as pltpu
from jax.sharding import PartitionSpec as P

HEAD_DIM = 64
SPAN = 256
F32 = jnp.float32
BF16 = jnp.bfloat16
ROWS = 8
LANES = 128
NOTE = 16
SEQ, CORE, PLACE = 0, 1, 2


def iota(shape, axis):
    return lax.broadcasted_iota(jnp.int32, shape, axis)


IN_HBM = pl.BlockSpec(memory_space=pltpu.HBM)
IN_SMEM = pl.BlockSpec(memory_space=pltpu.SMEM)
IN_VMEM = pl.BlockSpec(memory_space=pltpu.VMEM)


def shaped(shape, dtype):
    return pltpu.VMEM(shape, dtype)


def in_hbm(*arrays):
    return [pltpu.with_memory_space_constraint(array, pltpu.HBM) for array in arrays]


TAKES = {
    "join_projections": 1.7,
    "factors": 2.3,
    "scale_grad": 3.6,
    "scale_in": 0.01,
    "back_state": 1.1,
    "front_state": 0.01,
    "second_front": 0.7,
    "back_outputs": 3.4,
    "front_outputs": 3.4,
    "rest_gram": 2.4,
    "finish_in": 1.3,
    "finish_grad": 1.6,
}


def call(body, in_specs, out_shape, name, scratch=(), out_specs=None, mib=24):
    takes = TAKES[name]
    cost = pl.CostEstimate(
        flops=int(takes * 1.15e9), bytes_accessed=int(takes * 3.6e6), transcendentals=0
    )
    return pl.pallas_call(
        body,
        in_specs=[IN_SMEM] + in_specs,
        out_specs=out_specs or [IN_VMEM] * len(out_shape),
        out_shape=out_shape,
        scratch_shapes=list(scratch),
        compiler_params=pltpu.CompilerParams(vmem_limit_bytes=mib << 20),
        cost_estimate=cost,
        name=name,
    )


def dot(left, right, left_axis=1, right_axis=0):
    return lax.dot_general(
        left, right, (((left_axis,), (right_axis,)), ((), ())), preferred_element_type=F32
    )


def bits(count):
    if count & (count - 1):
        raise ValueError("power of 2")
    return count.bit_length() - 1


def spread(heads, width, first):
    lane = iota((LANES, width), 0)
    hit = (lane & (heads - 1)) == (iota((LANES, width), 1) >> bits(HEAD_DIM))
    group = lane >> bits(heads)
    return (hit & ((group >> 1) == first // 2)).astype(F32).astype(BF16)


def copies(heads):
    lane = iota((heads, LANES), 1)
    hit = ((lane & (heads - 1)) == iota((heads, LANES), 0)) & (lane < 4 * heads)
    return hit.astype(F32).astype(BF16)


def split_parts(values, heads):
    high = values.astype(BF16)
    low = (values - high.astype(F32)).astype(BF16)
    is_low = ((iota(values.shape, 1) >> bits(heads)) & 1) == 1
    return jnp.where(is_low, low.astype(F32), high.astype(F32)).astype(BF16)


def join_body(at_ref, b_hbm, c_hbm, keep_hbm, step_hbm, out_ref, note_ref, keep_ref, step_ref, arrived):
    state = b_hbm.shape[1]
    moves = [
        pltpu.make_async_copy(keep_hbm, keep_ref, arrived.at[0]),
        pltpu.make_async_copy(b_hbm, out_ref.at[:, pl.ds(0, state)], arrived.at[1]),
        pltpu.make_async_copy(c_hbm, out_ref.at[:, pl.ds(state, state)], arrived.at[2]),
        pltpu.make_async_copy(step_hbm, step_ref, arrived.at[3]),
    ]
    for move in moves:
        move.start()
    heads = keep_ref.shape[0]
    copied = copies(heads)
    moves[0].wait()
    logs = jnp.sum(dot(keep_ref[...], copied, 0, 0), axis=0, keepdims=True)
    note_ref[...] = split_parts(jnp.exp(jnp.broadcast_to(logs, note_ref.shape)), heads)
    for move in moves[1:]:
        move.wait()


def join(at, b_proj, c_proj, keep, step):
    rows, state = b_proj.shape
    return call(
        join_body,
        [IN_HBM] * 4,
        [
            shaped((rows, 2 * state), BF16),
            shaped((NOTE, LANES), BF16),
            shaped(keep.shape, BF16),
            shaped(step.shape, BF16),
        ],
        "join_projections",
        [pltpu.SemaphoreType.DMA((4,))],
    )(at, *in_hbm(b_proj, c_proj, keep, step))


def factors_body(at_ref, keep_ref, step_ref, packed_ref, decay_ref):
    heads, rows = keep_ref.shape
    width = decay_ref.shape[1]
    lower = (iota((SPAN, SPAN), 0) >= iota((SPAN, SPAN), 1)).astype(F32).astype(BF16)
    take_u, copied = spread(heads, width, 0), copies(heads)
    group = iota((SPAN, LANES), 1) >> bits(heads)
    row = iota((ROWS, LANES), 0)
    for block in range(rows // SPAN):
        cut = slice(block * SPAN, (block + 1) * SPAN)
        keep = dot(keep_ref[:, cut], copied, 0, 0).astype(BF16)
        step = dot(step_ref[:, cut], copied, 0, 0)
        cum = dot(lower, keep)
        mid = cum[SPAN // 2 - 1 : SPAN // 2]
        end = cum[SPAN - 1 : SPAN]
        offset = cum - mid
        factor = jnp.exp(jnp.where(group < 2, offset, -offset)) * jnp.where(group < 2, 1.0, step)
        packed_ref[cut] = split_parts(factor, heads)
        logs = jnp.where(row == 0, mid, jnp.where(row == 1, end - mid, end))
        decay_ref[block * ROWS : (block + 1) * ROWS] = dot(split_parts(jnp.exp(logs), heads), take_u)


def factors(at, keep, step):
    heads, rows = keep.shape
    return call(
        factors_body,
        [IN_VMEM] * 2,
        [shaped((rows, LANES), BF16), shaped((rows // SPAN * ROWS, heads * HEAD_DIM), F32)],
        "factors",
    )(at, keep, step)


def scale_body(at_ref, value_hbm, *rest, first):
    if len(rest) == 4:
        packed_ref, out_ref, value_ref, arrived = rest
    else:
        layer_hbm, packed_ref, out_ref, in_x, in_y, in_kx, in_ky, gram_ref, layer_ref, value_ref, arrived = rest
    rows, width = value_ref.shape
    blocks = rows // SPAN
    moves = []
    for block in range(blocks):
        cut = pl.ds(block * SPAN, SPAN)
        moves.append(pltpu.make_async_copy(value_hbm.at[cut, :], value_ref.at[cut, :], arrived.at[block]))
    if len(rest) > 4:
        moves.append(pltpu.make_async_copy(layer_hbm, layer_ref, arrived.at[blocks]))
    for move in moves:
        move.start()
    taken = spread(width // HEAD_DIM, width, first)
    for block in range(blocks):
        cut = slice(block * SPAN, (block + 1) * SPAN)
        moves[block].wait()
        out_ref[cut] = (value_ref[cut].astype(F32) * dot(packed_ref[cut], taken)).astype(BF16)
    if len(rest) == 4:
        return
    moves[-1].wait()
    width = layer_ref.shape[1]
    part, half = width // 4, width // 2
    gram_ref[...] = dot(layer_ref[...], layer_ref[...], 0, 0).astype(BF16)
    for flip, left, right, at in ((1, in_x, in_ky, (0, 1)), (3, in_x, in_y, (1, 1)), (2, in_kx, in_y, (1, 0)),
                                  (0, in_kx, in_ky, (0, 0))):
        start = pl.multiple_of((at_ref[SEQ] ^ flip) * part, part)
        rows_of = gram_ref[pl.ds(start, part), :]
        left[at[0] * part : (at[0] + 1) * part] = rows_of[:, :half]
        right[at[1] * part : (at[1] + 1) * part] = rows_of[:, half:]


def scale(at, values, packed, first, layer_input=None):
    rows, width = values.shape
    hbm, out_shape = [values], [shaped((rows, width), BF16)]
    scratch = [pltpu.VMEM((rows, width), BF16), pltpu.SemaphoreType.DMA((rows // SPAN + 1,))]
    if layer_input is not None:
        cols = layer_input.shape[1]
        hbm.append(layer_input)
        out_shape += [shaped((cols // 2, cols // 2), BF16)] * 4
        scratch = [pltpu.VMEM((cols, cols), BF16), pltpu.VMEM(layer_input.shape, BF16)] + scratch
    return call(
        functools.partial(scale_body, first=first),
        [IN_HBM] * len(hbm) + [IN_VMEM],
        out_shape,
        "scale_grad" if first == 0 else "scale_in",
        scratch,
    )(at, *in_hbm(*hbm), packed)


def block_rows(at_ref, mine_ref, other_ref, block, side=None):
    swap = at_ref[CORE] == 1
    place = at_ref[PLACE + block]
    state = mine_ref.shape[2] // 2
    cols = slice(None) if side is None else slice(side * state, (side + 1) * state)
    mine, other = mine_ref[place][:, cols], other_ref[place][:, cols]
    return jnp.concatenate([jnp.where(swap, other, mine), jnp.where(swap, mine, other)], axis=0)


def state_body(at_ref, mine_ref, other_ref, val_ref, decay_ref, *rest, backward):
    (own_ref, total_ref), rest = (rest[:2], rest[2:]) if backward else (rest[1:3], rest[:1] + rest[3:])
    width = val_ref.shape[1]
    state = mine_ref.shape[2] // 2
    blocks = val_ref.shape[0] // SPAN
    pick = 0 if backward else 1
    carry = mine = None
    for block in reversed(range(blocks)) if backward else range(blocks):
        rows = block_rows(at_ref, mine_ref, other_ref, block, 1 if backward else 0)
        at = block * ROWS
        own = dot(rows, val_ref[block * SPAN : (block + 1) * SPAN], 0, 0)
        own = own * decay_ref[at + pick : at + pick + 1]
        own_ref[block * state : (block + 1) * state] = own
        decay = decay_ref[at + 2 : at + 3]
        carry = own if carry is None else carry * decay + own
        mine = decay if mine is None else mine * decay
    total_ref[...] = carry.astype(BF16)
    if backward:
        return
    note_ref, first_ref, back_ref, front_ref = rest
    near = dot(note_ref[...], spread(width // HEAD_DIM, width, 0))[0:1]
    one, zero = jnp.ones_like(mine), jnp.zeros_like(mine)

    def choose(place, *rows):
        picked = zero
        for at, row in enumerate(rows):
            picked = jnp.where(place == at, row, picked)
        return picked

    place = at_ref[SEQ]
    back_ref[...] = jnp.zeros_like(back_ref)
    back_ref[0:1] = choose(place, zero, zero, one, near)
    back_ref[1:2] = choose(place, zero, zero, mine, one)
    back_ref[2:3] = choose(place, one, zero, one, zero)
    back_ref[3:4] = choose(place, near, one, zero, zero)
    place = 3 - at_ref[SEQ]
    front_ref[...] = jnp.zeros_like(front_ref)
    front_ref[0:1] = choose(place, zero, one, zero, one)
    front_ref[1:2] = choose(place, one, mine, zero, zero)
    front_ref[2:3] = choose(place, near, one, zero, zero)
    front_ref[3:4] = choose(place, one, one, one, zero)
    first_ref[...] = (carry * choose(place, one, one, one, near)).astype(BF16)


def fold(value, times):
    rows = value.shape[0] // times
    return jnp.concatenate([value[at * rows : (at + 1) * rows] for at in range(times)], axis=1)


def unfold(value, times):
    cols = value.shape[1] // times
    return jnp.concatenate([value[:, at * cols : (at + 1) * cols] for at in range(times)], axis=0)


def device_state(at, gathered, values, decays, note=None):
    rows, width = values.shape
    state = gathered[0].shape[2] // 2
    blocks = rows // SPAN
    backward = note is None
    total, mix = shaped((state, width), BF16), shaped((ROWS, width), F32)
    return call(
        functools.partial(state_body, backward=backward),
        [IN_VMEM] * (4 if backward else 5),
        [shaped((blocks * state, width), F32), total] + ([] if backward else [total, mix, mix]),
        "back_state" if backward else "front_state",
    )(at, *gathered, values, decays, *([] if backward else [note]))


def second_body(at_ref, own_ref, got_ref, mix_ref, in_ky, in_y1, out_ref):
    part = in_ky.shape[0] // 2
    state = own_ref.shape[0]
    mixed = own_ref[...].astype(F32) * mix_ref[0:1] + got_ref[...].astype(F32) * mix_ref[1:2]
    out_ref[:state] = mixed.astype(BF16)
    out_ref[state:] = fold(in_ky[part:].astype(F32) + in_y1[part:].astype(F32), 4).astype(BF16)


def second_front(at, own, got, mix, in_ky, in_y1):
    state, width = own.shape
    shape = (state + in_ky.shape[0] // 8, width)
    return call(second_body, [IN_VMEM] * 5, [shaped(shape, BF16)], "second_front")(
        at, own, got, mix, in_ky, in_y1
    )[0]


def outputs_body(
    at_ref, mine_ref, other_ref, val_ref, packed_ref, decay_ref, own_ref, early, late, mix_ref, out_hbm, *rest,
    backward, square,
):
    (kept, *gram_refs), left = (rest[:-1], rest[-1])
    width = val_ref.shape[1]
    heads = width // HEAD_DIM
    state = mine_ref.shape[2] // 2
    blocks = val_ref.shape[0] // SPAN
    pick = 1 if backward else 0
    taken = spread(heads, width, 2 if backward else 0)
    down, across = iota((SPAN, SPAN), 0), iota((SPAN, SPAN), 1)
    keep = down <= across if backward else down >= across
    entering = early[:state].astype(F32) * mix_ref[2:3] + late[:state].astype(F32) * mix_ref[3:4]
    moves = []
    for block in reversed(range(blocks)) if backward else range(blocks):
        cut = slice(block * SPAN, (block + 1) * SPAN)
        at = block * ROWS
        proj = block_rows(at_ref, mine_ref, other_ref, block)
        b_rows, c_rows = proj[:, :state], proj[:, state:]
        rows_of, cols_of = (b_rows, c_rows) if backward else (c_rows, b_rows)
        score = jnp.where(keep, dot(rows_of, cols_of, 1, 1), 0.0).astype(BF16)
        total = dot(score, val_ref[cut]) + dot(
            rows_of, (entering * decay_ref[at + pick : at + pick + 1]).astype(BF16)
        )
        kept[cut] = (total * dot(packed_ref[cut], taken)).astype(BF16)
        rows = pl.ds(block * SPAN, SPAN)
        moves.append(pltpu.make_async_copy(kept.at[rows, :], out_hbm.at[rows, :], left.at[block]))
        moves[-1].start()
        entering = entering * decay_ref[at + 2 : at + 3] + own_ref[block * state : (block + 1) * state]
    if gram_refs:
        gram_rows(at_ref, kept, ((3, *gram_refs),))
    for move in moves:
        move.wait()


def gram_rows(at_ref, rows_ref, wanted):
    width = rows_ref.shape[1]
    part, half = width // 4, width // 2
    for flip, left, right in wanted:
        start = pl.multiple_of((at_ref[SEQ] ^ flip) * part, part)
        gram = dot(rows_ref[:, pl.ds(start, part)], rows_ref[...], 0, 0)
        left[:part] = gram[:, :half].astype(BF16)
        right[:part] = gram[:, half:].astype(BF16)


def outputs(at, gathered, values, packed, decays, own, early, late, mix, backward, square=True):
    rows, width = values.shape
    out_shape = [pltpu.HBM((rows, width), BF16)]
    scratch = [pltpu.SemaphoreType.DMA((rows // SPAN,))]
    if backward and square:
        out_shape += [shaped((rows, width), BF16)] + [shaped((width // 4, width // 2), BF16)] * 2
    else:
        scratch = [pltpu.VMEM((rows, width), BF16)] + scratch
    return call(
        functools.partial(outputs_body, backward=backward, square=square),
        [IN_VMEM] * 9,
        out_shape,
        "back_outputs" if backward else "front_outputs",
        scratch,
        [IN_HBM] + [IN_VMEM] * (len(out_shape) - 1),
    )(at, *gathered, values, packed, decays, own, early, late, mix)


def rest_body(at_ref, rows_ref, in_kx, in_x1, x1, y2, x0, x2, y0, y1):
    part = rows_ref.shape[1] // 4
    in_part = in_kx.shape[0] // 2
    y2[part:] = fold(in_kx[in_part:].astype(F32) + in_x1[in_part:].astype(F32), 2).astype(BF16)
    gram_rows(at_ref, rows_ref, ((1, x1, y1), (2, x2, y2), (0, x0, y0)))


def rest_gram(at, x_grad, in_kx, in_x1):
    width = x_grad.shape[1]
    part = shaped((width // 4, width // 2), BF16)
    sent = shaped((width // 4 + in_kx.shape[0] // 4, width // 2), BF16)
    return call(rest_body, [IN_VMEM] * 3, [part, sent] + [part] * 4, "rest_gram")(at, x_grad, in_kx, in_x1)


def finish_body(at_ref, *refs, scale):
    parts, (out_hbm, out_ref, left) = refs[:6], refs[6:]
    rows, width = out_ref.shape
    half = width // 2
    moves = []
    for side in range(2):
        one, two, three = parts[3 * side : 3 * side + 3]
        last = three[...]
        if last.shape[1] != half:
            times = last.shape[1] // half
            last = unfold(last[last.shape[0] - rows // times :].astype(F32), times)
        cols = pl.ds(side * half, half)
        out_ref[:, cols] = (one[:rows].astype(F32) + two[:rows].astype(F32) + last.astype(F32)) * scale
        moves.append(pltpu.make_async_copy(out_ref.at[:, cols], out_hbm.at[:, cols], left.at[side]))
        moves[-1].start()
    for move in moves:
        move.wait()


def finish(at, left, right, shape, seq_total, name):
    return call(
        functools.partial(finish_body, scale=1.0 / seq_total),
        [IN_VMEM] * 6,
        [pltpu.HBM(shape, F32)],
        name,
        [pltpu.VMEM(shape, F32), pltpu.SemaphoreType.DMA((2,))],
        [IN_HBM],
    )(at, *left, *right)[0]


def after(value, *others):
    return lax.optimization_barrier((value, *others))[0]


def gather_rows(rows_in, *others):
    mp_count = lax.axis_size("mp")
    pieces = [rows_in]
    for shift in range(1, mp_count // 2):
        perm = [(m, (m + 2 * shift) % mp_count) for m in range(mp_count)]
        pieces.append(lax.ppermute(rows_in, "mp", perm))
    mine = after(jnp.stack(pieces), *others)
    return mine, lax.ppermute(mine, "mp", [(m, m ^ 1) for m in range(mp_count)])


def order_rows(mine, other):
    z_count, count, width = mine.shape
    z_at, core = lax.axis_index("mp") // 2, lax.axis_index("mp") % 2
    order = (z_at - jnp.arange(z_count)) % z_count
    pair = jnp.where(core == 0, jnp.stack([mine, other], axis=1), jnp.stack([other, mine], axis=1))
    rows = pair[order].reshape(-1, 2, SPAN // 2, width)
    return rows[:, 0], rows[:, 1]


X_PAIRS = [(0, 1), (1, 0), (2, 3), (3, 2)]
Y_PAIRS = [(0, 2), (2, 0), (1, 3), (3, 1)]


def go(value, pairs):
    return lax.ppermute(value, "seq", pairs)


def added(one, two):
    return (one.astype(F32) + two.astype(F32)).astype(BF16)


def second_message(own, got, mix):
    return (own.astype(F32) * mix[0:1] + got.astype(F32) * mix[1:2]).astype(BF16)


def square_shards(x_in, step_size, log_keep, b_proj, c_proj, y_grad, layer_input):
    tok_rows, width = x_in.shape
    seq_total = tok_rows * 4
    z_count = lax.axis_size("mp") // 2
    z_at, core = lax.axis_index("mp") // 2, lax.axis_index("mp") % 2
    direct = b_proj.shape[0] * 2 == SPAN
    places = jnp.arange(tok_rows // SPAN)
    if direct:
        places = (z_at - places) % z_count
    at = jnp.concatenate([jnp.stack([lax.axis_index("seq"), core if direct else 0]), places])
    at = at.astype(jnp.int32)

    joined, note, keep, step = join(at, b_proj, c_proj, log_keep.T, step_size.T)
    note = go(note, X_PAIRS)
    packed, decays = factors(at, keep, step)
    gu, in_x, in_y, in_kx, in_ky = scale(at, y_grad, after(packed, note), 0, layer_input)
    gathered = gather_rows(joined, gu)
    if not direct:
        gathered = order_rows(*gathered)
    own_back, back = device_state(at, gathered, gu, decays)
    back_one = go(back, [(1, 0), (3, 2), (2, 3)])
    in_y1 = go(in_y, Y_PAIRS)
    xv = scale(at, x_in, after(packed, own_back), 2)[0]
    own_front, front, front_first, back_mix, front_mix = device_state(
        at, gathered, after(xv, in_y1), decays, note
    )
    front_one = go(front_first, Y_PAIRS)
    back_send = second_message(back, back_one, back_mix)
    back_two = go(back_send, [(2, 0), (3, 1)])
    in_x1 = go(after(in_x, back_send), X_PAIRS)
    front_send = second_front(at, front, front_one, front_mix, in_ky, in_y1)
    front_two = go(front_send, X_PAIRS)

    x_grad, kept, x3, y3 = outputs(
        at, gathered, after(gu, front_send, in_x1), packed, decays, own_back, back_one, back_two, back_mix, True
    )

    x3_in, y3_in = go(x3, X_PAIRS), go(y3, Y_PAIRS)
    x1, y2, x0, x2, y0, y1 = rest_gram(at, after(kept, front_two), in_kx, in_x1)
    x1_in, y2_in = go(x1, X_PAIRS), go(y2, Y_PAIRS)
    x_two = go(added(x3_in, x2), Y_PAIRS)
    y_two = go(added(y3_in, y1), X_PAIRS)
    y_out = outputs(
        at, gathered, xv, packed, decays, own_front, front_one, front_two, front_mix, False
    )[0]
    in_shape = (layer_input.shape[1] // 4, layer_input.shape[1])
    in_factor = finish(
        at, (in_kx, in_x1, y2_in[width // 4 :]), (in_ky, in_y1, front_two), in_shape, seq_total, "finish_in"
    )
    grad_factor = finish(
        at, (x0, x1_in, x_two), (y0, y2_in, y_two), (width // 4, width), seq_total, "finish_grad"
    )
    return (y_out, x_grad, in_factor, grad_factor)


def enter_any(total, decay_all, seq_at, backward):
    seq_count = decay_all.shape[0]
    width = total.shape[1]
    totals = lax.all_gather(total, "seq")
    if not backward:
        totals, decay_all, seq_at = totals[::-1], decay_all[::-1], seq_count - 1 - seq_at
    entering = jnp.zeros(total.shape, F32)
    for at in range(seq_count - 1, 0, -1):
        moved = jnp.repeat(decay_all[at], HEAD_DIM) * entering + totals[at].astype(F32)
        entering = jnp.where(at > seq_at, moved, entering)
    high = entering.astype(BF16)
    low = (entering - high.astype(F32)).astype(BF16)
    return high, low, jnp.ones((ROWS, width), F32)


def summed(rows, seq_total):
    gram = dot(rows, rows, 0, 0).astype(BF16)
    total = lax.psum_scatter(gram, "seq", scatter_dimension=0, tiled=True)
    return total.astype(F32) / seq_total


def any_shards(x_in, step_size, log_keep, b_proj, c_proj, y_grad, layer_input):
    tok_rows, width = x_in.shape
    heads = step_size.shape[1]
    seq_total = tok_rows * lax.axis_size("seq")
    seq_at = lax.axis_index("seq")
    at = jnp.concatenate([jnp.zeros((2,), jnp.int32), jnp.arange(tok_rows // SPAN, dtype=jnp.int32)])
    note = jnp.zeros((NOTE, LANES), BF16)
    decay_all = lax.all_gather(jnp.exp(jnp.sum(log_keep.astype(F32), axis=0)), "seq")
    joined, _, keep, step = join(at, b_proj, c_proj, log_keep.T, step_size.T)
    gathered = order_rows(*gather_rows(joined))
    packed, decays = factors(at, keep, step)
    gu, xv = scale(at, y_grad, packed, 0)[0], scale(at, x_in, packed, 2)[0]
    results = []
    for values, backward in ((gu, True), (xv, False)):
        own, total, *_ = device_state(at, gathered, values, decays, None if backward else note)
        early, late, mix = enter_any(total, decay_all, seq_at, backward)
        results.append(
            outputs(at, gathered, values, packed, decays, own, early, late, mix, backward, False)[0]
        )
    x_grad, y_out = results
    return (y_out, x_grad, summed(layer_input, seq_total), summed(x_grad, seq_total))


def solution(mesh):
    spec = P("seq", "mp")
    rows = P(("seq", "mp"), None)
    return jax.shard_map(
        square_shards if mesh.shape["seq"] == 4 else any_shards,
        mesh=mesh,
        in_specs=(spec, spec, spec, rows, rows, spec, spec),
        out_specs=(spec, spec, spec, spec),
        check_vma=False,
    )
```

```python
import functools

import jax
import jax.numpy as jnp
import numpy as np
from jax import lax
from jax.experimental import pallas as pl
from jax.experimental.pallas import tpu as pltpu
from jax.sharding import PartitionSpec as P

HEAD_DIM = 64
SPAN = 256
F32 = jnp.float32
BF16 = jnp.bfloat16
ROWS = 8
LANES = 128
NOTE = 16
SEQ, CORE, PLACE = 0, 1, 2


def iota(shape, axis):
    return lax.broadcasted_iota(jnp.int32, shape, axis)


IN_HBM = pl.BlockSpec(memory_space=pltpu.HBM)
IN_SMEM = pl.BlockSpec(memory_space=pltpu.SMEM)
IN_VMEM = pl.BlockSpec(memory_space=pltpu.VMEM)


def shaped(shape, dtype):
    return pltpu.VMEM(shape, dtype)


def in_hbm(*arrays):
    return [pltpu.with_memory_space_constraint(array, pltpu.HBM) for array in arrays]


TAKES = {
    "join_projections": 1.7,
    "prepare": 5.5,
    "in_gram": 2.0,
    "states": 2.2,
    "back_outputs": 3.4,
    "front_outputs": 3.4,
    "rest_gram": 2.4,
    "finish_in": 1.3,
    "finish_grad": 1.6,
}


def call(body, in_specs, out_shape, name, scratch=(), out_specs=None, mib=24):
    takes = TAKES[name]
    cost = pl.CostEstimate(
        flops=int(takes * 1.15e9), bytes_accessed=int(takes * 3.6e6), transcendentals=0
    )
    return pl.pallas_call(
        body,
        in_specs=[IN_SMEM] + in_specs,
        out_specs=out_specs or [IN_VMEM] * len(out_shape),
        out_shape=out_shape,
        scratch_shapes=list(scratch),
        compiler_params=pltpu.CompilerParams(vmem_limit_bytes=mib << 20),
        cost_estimate=cost,
        name=name,
    )


def dot(left, right, left_axis=1, right_axis=0):
    return lax.dot_general(
        left, right, (((left_axis,), (right_axis,)), ((), ())), preferred_element_type=F32
    )


def bits(count):
    if count & (count - 1):
        raise ValueError("power of 2")
    return count.bit_length() - 1


def spread(heads, width, first):
    lane = iota((LANES, width), 0)
    hit = (lane & (heads - 1)) == (iota((LANES, width), 1) >> bits(HEAD_DIM))
    group = lane >> bits(heads)
    return (hit & ((group >> 1) == first // 2)).astype(F32).astype(BF16)


def copies(heads):
    lane = iota((heads, LANES), 1)
    hit = ((lane & (heads - 1)) == iota((heads, LANES), 0)) & (lane < 4 * heads)
    return hit.astype(F32).astype(BF16)


def split_parts(values, heads):
    high = values.astype(BF16)
    low = (values - high.astype(F32)).astype(BF16)
    is_low = ((iota(values.shape, 1) >> bits(heads)) & 1) == 1
    return jnp.where(is_low, low.astype(F32), high.astype(F32)).astype(BF16)


def join_body(at_ref, b_hbm, c_hbm, keep_hbm, step_hbm, out_ref, keep_ref, step_ref, arrived):
    state = b_hbm.shape[1]
    moves = [
        pltpu.make_async_copy(b_hbm, out_ref.at[:, pl.ds(0, state)], arrived.at[0]),
        pltpu.make_async_copy(c_hbm, out_ref.at[:, pl.ds(state, state)], arrived.at[1]),
        pltpu.make_async_copy(keep_hbm, keep_ref, arrived.at[2]),
        pltpu.make_async_copy(step_hbm, step_ref, arrived.at[3]),
    ]
    for move in moves:
        move.start()
    for move in moves:
        move.wait()


def join(at, b_proj, c_proj, keep, step):
    rows, state = b_proj.shape
    return call(
        join_body,
        [IN_HBM] * 4,
        [shaped((rows, 2 * state), BF16), shaped(keep.shape, BF16), shaped(step.shape, BF16)],
        "join_projections",
        [pltpu.SemaphoreType.DMA((4,))],
    )(at, *in_hbm(b_proj, c_proj, keep, step))


def prepare_body(
    at_ref, g_hbm, x_hbm, keep_ref, step_ref, gu_ref, xv_ref, packed_ref, decay_ref, g_ref, x_ref, arrived
):
    rows, width = g_ref.shape
    heads = keep_ref.shape[0]
    blocks = rows // SPAN
    cuts = [slice(block * SPAN, (block + 1) * SPAN) for block in range(blocks)]
    moves = []
    for hbm, ref in ((g_hbm, g_ref), (x_hbm, x_ref)):
        for block in range(blocks):
            cut = pl.ds(block * SPAN, SPAN)
            moves.append(pltpu.make_async_copy(hbm.at[cut, :], ref.at[cut, :], arrived.at[len(moves)]))
    for move in moves:
        move.start()
    lower = (iota((SPAN, SPAN), 0) >= iota((SPAN, SPAN), 1)).astype(F32).astype(BF16)
    take_u, take_v, copied = spread(heads, width, 0), spread(heads, width, 2), copies(heads)
    keep = dot(keep_ref[...], copied, 0, 0).astype(BF16)
    step = dot(step_ref[...], copied, 0, 0)
    cums = [dot(lower, keep[cut]) for cut in cuts]
    mids = [cum[SPAN // 2 - 1 : SPAN // 2] for cum in cums]
    ends = [cum[SPAN - 1 : SPAN] for cum in cums]
    offset = jnp.concatenate([cum - mid for cum, mid in zip(cums, mids)], axis=0)
    on_u = (iota((rows, LANES), 1) >> bits(heads)) < 2
    factor = jnp.exp(jnp.where(on_u, offset, -offset)) * jnp.where(on_u, 1.0, step)
    packed_ref[...] = split_parts(factor, heads)
    row = iota((ROWS, LANES), 0)
    logs = [jnp.where(row == 0, mid, jnp.where(row == 1, end - mid, end)) for mid, end in zip(mids, ends)]
    decay_ref[...] = dot(split_parts(jnp.exp(jnp.concatenate(logs, axis=0)), heads), take_u)
    for first, (ref, taken, out_ref) in enumerate(((g_ref, take_u, gu_ref), (x_ref, take_v, xv_ref))):
        for block, cut in enumerate(cuts):
            moves[first * blocks + block].wait()
            out_ref[cut] = (ref[cut].astype(F32) * dot(packed_ref[cut], taken)).astype(BF16)


def prepare(at, y_grad, x_in, keep, step):
    rows, width = x_in.shape
    blocks = rows // SPAN
    wide = shaped((rows, width), BF16)
    return call(
        prepare_body,
        [IN_HBM] * 2 + [IN_VMEM] * 2,
        [wide, wide, shaped((rows, LANES), BF16), shaped((blocks * ROWS, width), F32)],
        "prepare",
        [wide, wide, pltpu.SemaphoreType.DMA((2 * blocks,))],
    )(at, *in_hbm(y_grad, x_in), keep, step)


def in_gram_body(at_ref, layer_hbm, in_x, in_y, in_kx, in_ky, gram_ref, layer_ref, arrived):
    move = pltpu.make_async_copy(layer_hbm, layer_ref, arrived.at[0])
    move.start()
    move.wait()
    width = layer_ref.shape[1]
    part, half = width // 4, width // 2
    gram_ref[...] = dot(layer_ref[...], layer_ref[...], 0, 0).astype(BF16)
    places = ((1, in_x, 0, in_ky, 1), (3, in_x, 1, in_y, 1), (2, in_kx, 1, in_y, 0), (0, in_kx, 0, in_ky, 0))
    for flip, left, left_at, right, right_at in places:
        start = pl.multiple_of((at_ref[SEQ] ^ flip) * part, part)
        rows_of = gram_ref[pl.ds(start, part), :]
        left[left_at * part : (left_at + 1) * part] = rows_of[:, :half]
        right[right_at * part : (right_at + 1) * part] = rows_of[:, half:]


def in_gram(at, layer_input):
    cols = layer_input.shape[1]
    return call(
        in_gram_body,
        [IN_HBM],
        [shaped((cols // 2, cols // 2), BF16)] * 4,
        "in_gram",
        [shaped((cols, cols), BF16), shaped(layer_input.shape, BF16), pltpu.SemaphoreType.DMA((1,))],
    )(at, *in_hbm(layer_input))


def block_rows(at_ref, mine_ref, other_ref, block, side=None):
    swap = at_ref[CORE] == 1
    place = at_ref[PLACE + block]
    state = mine_ref.shape[2] // 2
    cols = slice(None) if side is None else slice(side * state, (side + 1) * state)
    mine, other = mine_ref[place][:, cols], other_ref[place][:, cols]
    return jnp.concatenate([jnp.where(swap, other, mine), jnp.where(swap, mine, other)], axis=0)


def state_body(at_ref, mine_ref, other_ref, gu_ref, xv_ref, decay_ref, back_ref, front_ref, *sent_refs):
    state = mine_ref.shape[2] // 2
    blocks = gu_ref.shape[0] // SPAN
    totals = []
    for val_ref, own_ref, side in ((gu_ref, back_ref, 1), (xv_ref, front_ref, 0)):
        carry = mine = None
        for block in reversed(range(blocks)) if side else range(blocks):
            rows = block_rows(at_ref, mine_ref, other_ref, block, side)
            at = block * ROWS
            own = dot(rows, val_ref[block * SPAN : (block + 1) * SPAN], 0, 0)
            own = own * decay_ref[at + 1 - side : at + 2 - side]
            own_ref[block * state : (block + 1) * state] = own
            decay = decay_ref[at + 2 : at + 3]
            carry = own if carry is None else carry * decay + own
            mine = decay if mine is None else mine * decay
        totals.append(carry)
    back, front = totals
    if len(sent_refs) == 2:
        sent_refs[0][...] = back.astype(BF16)
        sent_refs[1][...] = front.astype(BF16)
        return
    high = mine.astype(BF16).astype(F32)
    row = iota((NOTE, mine.shape[1]), 0)
    note = jnp.where(row == 0, high, jnp.where(row == 1, mine - high, 0.0)).astype(BF16)
    back, front = back.astype(BF16), front.astype(BF16)
    for flip, ref in zip((3, 2, 1), sent_refs):
        to_earlier = (at_ref[SEQ] ^ flip) < at_ref[SEQ]
        ref[:state] = jnp.where(to_earlier, back, front)
        ref[state:] = note


def fold(value, times):
    rows = value.shape[0] // times
    return jnp.concatenate([value[at * rows : (at + 1) * rows] for at in range(times)], axis=1)


def unfold(value, times):
    cols = value.shape[1] // times
    return jnp.concatenate([value[:, at * cols : (at + 1) * cols] for at in range(times)], axis=0)


def device_states(at, gathered, gu, xv, decays, square):
    rows, width = gu.shape
    state = gathered[0].shape[2] // 2
    own = shaped((rows // SPAN * state, width), F32)
    total = shaped((state, width), BF16)
    sent = [shaped((state + NOTE, width), BF16)] * 3 if square else [total, total]
    return call(state_body, [IN_VMEM] * 5, [own, own] + sent, "states")(at, *gathered, gu, xv, decays)


def enter(at_ref, refs, state, backward):
    notes = [ref[state:].astype(F32) for ref in refs]
    near_d, near_y, near_x = [note[0:1] + note[1:2] for note in notes]
    diagonal, along_y, along_x = [ref[:state].astype(F32) for ref in refs]
    one, zero = jnp.ones_like(near_x), jnp.zeros_like(near_x)
    place = at_ref[SEQ] if backward else 3 - at_ref[SEQ]

    def choose(*rows):
        picked = zero
        for at, row in enumerate(rows):
            picked = jnp.where(place == at, row, picked)
        return picked

    return (
        along_x * choose(one, zero, one, zero)
        + along_y * choose(near_x, near_d, zero, zero)
        + diagonal * choose(near_x * near_y, one, zero, zero)
    )


def outputs_body(
    at_ref, mine_ref, other_ref, val_ref, packed_ref, decay_ref, own_ref, *rest, backward, square
):
    got_count = 3 if square else 2
    got_refs, out_hbm, (kept, *gram_refs), left = rest[:got_count], rest[got_count], rest[got_count + 1 : -1], rest[-1]
    width = val_ref.shape[1]
    heads = width // HEAD_DIM
    state = mine_ref.shape[2] // 2
    blocks = val_ref.shape[0] // SPAN
    pick = 1 if backward else 0
    taken = spread(heads, width, 2 if backward else 0)
    down, across = iota((SPAN, SPAN), 0), iota((SPAN, SPAN), 1)
    keep = down <= across if backward else down >= across
    if square:
        entering = enter(at_ref, got_refs, state, backward)
    else:
        entering = got_refs[0][...].astype(F32) + got_refs[1][...].astype(F32)
    moves = []
    for block in reversed(range(blocks)) if backward else range(blocks):
        cut = slice(block * SPAN, (block + 1) * SPAN)
        at = block * ROWS
        proj = block_rows(at_ref, mine_ref, other_ref, block)
        b_rows, c_rows = proj[:, :state], proj[:, state:]
        rows_of, cols_of = (b_rows, c_rows) if backward else (c_rows, b_rows)
        score = jnp.where(keep, dot(rows_of, cols_of, 1, 1), 0.0).astype(BF16)
        total = dot(score, val_ref[cut]) + dot(
            rows_of, (entering * decay_ref[at + pick : at + pick + 1]).astype(BF16)
        )
        kept[cut] = (total * dot(packed_ref[cut], taken)).astype(BF16)
        rows = pl.ds(block * SPAN, SPAN)
        moves.append(pltpu.make_async_copy(kept.at[rows, :], out_hbm.at[rows, :], left.at[block]))
        moves[-1].start()
        entering = entering * decay_ref[at + 2 : at + 3] + own_ref[block * state : (block + 1) * state]
    if gram_refs:
        gram_rows(at_ref, kept, ((3, *gram_refs),))
    for move in moves:
        move.wait()


def gram_rows(at_ref, rows_ref, wanted):
    width = rows_ref.shape[1]
    part, half = width // 4, width // 2
    for flip, left, right in wanted:
        start = pl.multiple_of((at_ref[SEQ] ^ flip) * part, part)
        gram = dot(rows_ref[:, pl.ds(start, part)], rows_ref[...], 0, 0)
        left[:part] = gram[:, :half].astype(BF16)
        right[:part] = gram[:, half:].astype(BF16)


def outputs(at, gathered, values, packed, decays, own, got, backward, square=True):
    rows, width = values.shape
    out_shape = [pltpu.HBM((rows, width), BF16)]
    scratch = [pltpu.SemaphoreType.DMA((rows // SPAN,))]
    if backward and square:
        out_shape += [shaped((rows, width), BF16)] + [shaped((width // 4, width // 2), BF16)] * 2
    else:
        scratch = [pltpu.VMEM((rows, width), BF16)] + scratch
    return call(
        functools.partial(outputs_body, backward=backward, square=square),
        [IN_VMEM] * (6 + len(got)),
        out_shape,
        "back_outputs" if backward else "front_outputs",
        scratch,
        [IN_HBM] + [IN_VMEM] * (len(out_shape) - 1),
    )(at, *gathered, values, packed, decays, own, *got)


def rest_body(at_ref, rows_ref, in_kx, in_x1, in_ky, in_y1, x1, y2, x0, x2, y0, y1):
    part = rows_ref.shape[1] // 4
    half = in_kx.shape[0]
    for kept, got, out in ((in_kx, in_x1, y2), (in_ky, in_y1, x1)):
        out[part:] = fold(kept[half // 2 :].astype(F32) + got[half // 2 : half].astype(F32), 2).astype(BF16)
    gram_rows(at_ref, rows_ref, ((1, x1, y1), (2, x2, y2), (0, x0, y0)))


def rest_gram(at, x_grad, in_parts):
    width = x_grad.shape[1]
    part = shaped((width // 4, width // 2), BF16)
    sent = shaped((width // 4 + in_parts[0].shape[0] // 4, width // 2), BF16)
    return call(rest_body, [IN_VMEM] * 5, [sent] * 2 + [part] * 4, "rest_gram")(at, x_grad, *in_parts)


def finish_body(at_ref, *refs, scale):
    parts, (out_hbm, out_ref, left) = refs[:6], refs[6:]
    rows, width = out_ref.shape
    half = width // 2
    moves = []
    for side in range(2):
        one, two, three = parts[3 * side : 3 * side + 3]
        last = three[...]
        if last.shape[1] != half:
            times = last.shape[1] // half
            last = unfold(last[last.shape[0] - rows // times :].astype(F32), times)
        cols = pl.ds(side * half, half)
        out_ref[:, cols] = (one[:rows].astype(F32) + two[:rows].astype(F32) + last.astype(F32)) * scale
        moves.append(pltpu.make_async_copy(out_ref.at[:, cols], out_hbm.at[:, cols], left.at[side]))
        moves[-1].start()
    for move in moves:
        move.wait()


def finish(at, left, right, shape, seq_total, name):
    return call(
        functools.partial(finish_body, scale=1.0 / seq_total),
        [IN_VMEM] * 6,
        [pltpu.HBM(shape, F32)],
        name,
        [pltpu.VMEM(shape, F32), pltpu.SemaphoreType.DMA((2,))],
        [IN_HBM],
    )(at, *left, *right)[0]


def after(value, *others):
    return lax.optimization_barrier((value, *others))[0]


def gather_rows(rows_in, *others):
    mp_count = lax.axis_size("mp")
    pieces = [rows_in]
    for shift in range(1, mp_count // 2):
        perm = [(m, (m + 2 * shift) % mp_count) for m in range(mp_count)]
        pieces.append(lax.ppermute(rows_in, "mp", perm))
    mine = after(jnp.stack(pieces), *others)
    return mine, lax.ppermute(mine, "mp", [(m, m ^ 1) for m in range(mp_count)])


def order_rows(mine, other):
    z_count, count, width = mine.shape
    z_at, core = lax.axis_index("mp") // 2, lax.axis_index("mp") % 2
    order = (z_at - jnp.arange(z_count)) % z_count
    pair = jnp.where(core == 0, jnp.stack([mine, other], axis=1), jnp.stack([other, mine], axis=1))
    rows = pair[order].reshape(-1, 2, SPAN // 2, width)
    return rows[:, 0], rows[:, 1]


X_PAIRS = [(0, 1), (1, 0), (2, 3), (3, 2)]
Y_PAIRS = [(0, 2), (2, 0), (1, 3), (3, 1)]
D_PAIRS = [(0, 3), (3, 0), (1, 2), (2, 1)]


def go(value, pairs):
    return lax.ppermute(value, "seq", pairs)


def added(one, two):
    return (one.astype(F32) + two.astype(F32)).astype(BF16)


def square_shards(x_in, step_size, log_keep, b_proj, c_proj, y_grad, layer_input):
    tok_rows, width = x_in.shape
    seq_total = tok_rows * 4
    z_count = lax.axis_size("mp") // 2
    z_at, core = lax.axis_index("mp") // 2, lax.axis_index("mp") % 2
    direct = b_proj.shape[0] * 2 == SPAN
    places = jnp.arange(tok_rows // SPAN)
    if direct:
        places = (z_at - places) % z_count
    at = jnp.concatenate([jnp.stack([lax.axis_index("seq"), core if direct else 0]), places])
    at = at.astype(jnp.int32)

    joined, keep, step = join(at, b_proj, c_proj, log_keep.T, step_size.T)
    gu, xv, packed, decays = prepare(at, y_grad, x_in, keep, step)
    gathered = gather_rows(joined, decays)
    if not direct:
        gathered = order_rows(*gathered)

    own_back, own_front, diagonal, along_y, along_x = device_states(at, gathered, gu, xv, decays, True)
    diagonal, along_y, along_x = go(diagonal, D_PAIRS), go(along_y, Y_PAIRS), go(along_x, X_PAIRS)
    got = (diagonal, along_y, along_x)
    in_x, in_y, in_kx, in_ky = in_gram(at, after(layer_input, diagonal))
    in_x1, in_y1 = go(in_x, X_PAIRS), go(in_y, Y_PAIRS)
    x_grad, kept, x3, y3 = outputs(at, gathered, gu, packed, decays, own_back, got, True)

    x3_in, y3_in = go(x3, X_PAIRS), go(y3, Y_PAIRS)
    x1, y2, x0, x2, y0, y1 = rest_gram(at, kept, (in_kx, in_x1, in_ky, in_y1))
    x1_in, y2_in = go(x1, X_PAIRS), go(y2, Y_PAIRS)
    x_two = go(added(x3_in, x2), Y_PAIRS)
    y_two = go(added(y3_in, y1), X_PAIRS)
    y_out = outputs(at, gathered, xv, packed, decays, own_front, got, False)[0]
    in_shape = (layer_input.shape[1] // 4, layer_input.shape[1])
    in_second = (y2_in[width // 4 :], x1_in[width // 4 :])
    in_factor = finish(
        at, (in_kx, in_x1, in_second[0]), (in_ky, in_y1, in_second[1]), in_shape, seq_total, "finish_in"
    )
    grad_factor = finish(
        at, (x0, x1_in, x_two), (y0, y2_in, y_two), (width // 4, width), seq_total, "finish_grad"
    )
    return (y_out, x_grad, in_factor, grad_factor)


def enter_any(total, decay_all, seq_at, backward):
    seq_count = decay_all.shape[0]
    totals = lax.all_gather(total, "seq")
    if not backward:
        totals, decay_all, seq_at = totals[::-1], decay_all[::-1], seq_count - 1 - seq_at
    entering = jnp.zeros(total.shape, F32)
    for at in range(seq_count - 1, 0, -1):
        moved = jnp.repeat(decay_all[at], HEAD_DIM) * entering + totals[at].astype(F32)
        entering = jnp.where(at > seq_at, moved, entering)
    high = entering.astype(BF16)
    low = (entering - high.astype(F32)).astype(BF16)
    return high, low


def summed(rows, seq_total):
    gram = dot(rows, rows, 0, 0).astype(BF16)
    total = lax.psum_scatter(gram, "seq", scatter_dimension=0, tiled=True)
    return total.astype(F32) / seq_total


def any_shards(x_in, step_size, log_keep, b_proj, c_proj, y_grad, layer_input):
    tok_rows, width = x_in.shape
    heads = step_size.shape[1]
    seq_total = tok_rows * lax.axis_size("seq")
    seq_at = lax.axis_index("seq")
    at = jnp.concatenate([jnp.zeros((2,), jnp.int32), jnp.arange(tok_rows // SPAN, dtype=jnp.int32)])
    decay_all = lax.all_gather(jnp.exp(jnp.sum(log_keep.astype(F32), axis=0)), "seq")
    joined, keep, step = join(at, b_proj, c_proj, log_keep.T, step_size.T)
    gathered = order_rows(*gather_rows(joined))
    gu, xv, packed, decays = prepare(at, y_grad, x_in, keep, step)
    own_back, own_front, back, front = device_states(at, gathered, gu, xv, decays, False)
    results = []
    for values, own, total, backward in ((gu, own_back, back, True), (xv, own_front, front, False)):
        got = enter_any(total, decay_all, seq_at, backward)
        results.append(outputs(at, gathered, values, packed, decays, own, got, backward, False)[0])
    x_grad, y_out = results
    return (y_out, x_grad, summed(layer_input, seq_total), summed(x_grad, seq_total))


def solution(mesh):
    spec = P("seq", "mp")
    rows = P(("seq", "mp"), None)
    return jax.shard_map(
        square_shards if mesh.shape["seq"] == 4 else any_shards,
        mesh=mesh,
        in_specs=(spec, spec, spec, rows, rows, spec, spec),
        out_specs=(spec, spec, spec, spec),
        check_vma=False,
    )
```

```python
import functools

import jax
import jax.numpy as jnp
import numpy as np
from jax import lax
from jax.experimental import pallas as pl
from jax.experimental.pallas import tpu as pltpu
from jax.sharding import PartitionSpec as P

HEAD_DIM = 64
SPAN = 256
F32 = jnp.float32
BF16 = jnp.bfloat16
ROWS = 8
LANES = 128
NOTE = 8
PIECES = 4
SEQ, CORE, PLACE = 0, 1, 2


def iota(shape, axis):
    return lax.broadcasted_iota(jnp.int32, shape, axis)


IN_HBM = pl.BlockSpec(memory_space=pltpu.HBM)
IN_SMEM = pl.BlockSpec(memory_space=pltpu.SMEM)
IN_VMEM = pl.BlockSpec(memory_space=pltpu.VMEM)


def shaped(shape, dtype):
    return pltpu.VMEM(shape, dtype)


def in_hbm(*arrays):
    return [pltpu.with_memory_space_constraint(array, pltpu.HBM) for array in arrays]


TAKES = {
    "join_projections": 1.7,
    "prepare": 5.5,
    "in_gram": 1.3,
    "states": 2.2,
    "local_back": 3.0,
    "local_front": 3.0,
    "back_outputs": 2.5,
    "front_outputs": 2.0,
    "rest_gram": 2.4,
    "finish_in": 1.3,
    "middle": 1.0,
    "finish_grad": 1.6,
}


def call(body, in_specs, out_shape, name, scratch=(), out_specs=None, mib=24):
    takes = TAKES[name]
    cost = pl.CostEstimate(
        flops=int(takes * 1.15e9), bytes_accessed=int(takes * 3.6e6), transcendentals=0
    )
    return pl.pallas_call(
        body,
        in_specs=[IN_SMEM] + in_specs,
        out_specs=out_specs or [IN_VMEM] * len(out_shape),
        out_shape=out_shape,
        scratch_shapes=list(scratch),
        compiler_params=pltpu.CompilerParams(vmem_limit_bytes=mib << 20),
        cost_estimate=cost,
        name=name,
    )


def dot(left, right, left_axis=1, right_axis=0):
    return lax.dot_general(
        left, right, (((left_axis,), (right_axis,)), ((), ())), preferred_element_type=F32
    )


def bits(count):
    if count & (count - 1):
        raise ValueError("power of 2")
    return count.bit_length() - 1


def spread(heads, width, first):
    lane = iota((LANES, width), 0)
    hit = (lane & (heads - 1)) == (iota((LANES, width), 1) >> bits(HEAD_DIM))
    group = lane >> bits(heads)
    return (hit & ((group >> 1) == first // 2)).astype(F32).astype(BF16)


def copies(heads):
    lane = iota((heads, LANES), 1)
    hit = ((lane & (heads - 1)) == iota((heads, LANES), 0)) & (lane < 4 * heads)
    return hit.astype(F32).astype(BF16)


def split_parts(values, heads):
    high = values.astype(BF16)
    low = (values - high.astype(F32)).astype(BF16)
    is_low = ((iota(values.shape, 1) >> bits(heads)) & 1) == 1
    return jnp.where(is_low, low.astype(F32), high.astype(F32)).astype(BF16)


def join_body(at_ref, b_hbm, c_hbm, out_ref, arrived):
    state = b_hbm.shape[1]
    moves = [
        pltpu.make_async_copy(b_hbm, out_ref.at[:, pl.ds(0, state)], arrived.at[0]),
        pltpu.make_async_copy(c_hbm, out_ref.at[:, pl.ds(state, state)], arrived.at[1]),
    ]
    for move in moves:
        move.start()
    for move in moves:
        move.wait()


def join(at, b_proj, c_proj):
    rows, state = b_proj.shape
    return call(
        join_body,
        [IN_HBM] * 2,
        [shaped((rows, 2 * state), BF16)],
        "join_projections",
        [pltpu.SemaphoreType.DMA((2,))],
    )(at, *in_hbm(b_proj, c_proj))[0]


def prepare_body(
    at_ref, g_hbm, x_hbm, keep_hbm, step_hbm, layer_hbm, gu_ref, xv_ref, packed_ref, decay_ref, layer_ref,
    g_ref, x_ref, keep_ref, step_ref, arrived,
):
    rows, width = g_ref.shape
    heads = keep_ref.shape[0]
    blocks = rows // SPAN
    cuts = [slice(block * SPAN, (block + 1) * SPAN) for block in range(blocks)]
    thin = [
        pltpu.make_async_copy(keep_hbm, keep_ref, arrived.at[2 * blocks]),
        pltpu.make_async_copy(step_hbm, step_ref, arrived.at[2 * blocks + 1]),
    ]
    moves = []
    for hbm, ref in ((g_hbm, g_ref), (x_hbm, x_ref)):
        for block in range(blocks):
            cut = pl.ds(block * SPAN, SPAN)
            moves.append(pltpu.make_async_copy(hbm.at[cut, :], ref.at[cut, :], arrived.at[len(moves)]))
    layer_move = pltpu.make_async_copy(layer_hbm, layer_ref, arrived.at[2 * blocks + 2])
    for move in thin + moves + [layer_move]:
        move.start()
    lower = (iota((SPAN, SPAN), 0) >= iota((SPAN, SPAN), 1)).astype(F32).astype(BF16)
    take_u, take_v, copied = spread(heads, width, 0), spread(heads, width, 2), copies(heads)
    for move in thin:
        move.wait()
    keep = dot(keep_ref[...], copied, 0, 0).astype(BF16)
    step = dot(step_ref[...], copied, 0, 0)
    cums = [dot(lower, keep[cut]) for cut in cuts]
    mids = [cum[SPAN // 2 - 1 : SPAN // 2] for cum in cums]
    ends = [cum[SPAN - 1 : SPAN] for cum in cums]
    offset = jnp.concatenate([cum - mid for cum, mid in zip(cums, mids)], axis=0)
    on_u = (iota((rows, LANES), 1) >> bits(heads)) < 2
    factor = jnp.exp(jnp.where(on_u, offset, -offset)) * jnp.where(on_u, 1.0, step)
    packed_ref[...] = split_parts(factor, heads)
    row = iota((ROWS, LANES), 0)
    logs = [jnp.where(row == 0, mid, jnp.where(row == 1, end - mid, end)) for mid, end in zip(mids, ends)]
    decay_ref[...] = dot(split_parts(jnp.exp(jnp.concatenate(logs, axis=0)), heads), take_u)
    for first, (ref, taken, out_ref) in enumerate(((g_ref, take_u, gu_ref), (x_ref, take_v, xv_ref))):
        for block, cut in enumerate(cuts):
            moves[first * blocks + block].wait()
            out_ref[cut] = (ref[cut].astype(F32) * dot(packed_ref[cut], taken)).astype(BF16)
    layer_move.wait()


def prepare(at, y_grad, x_in, keep, step, layer_input):
    rows, width = x_in.shape
    blocks = rows // SPAN
    wide = shaped((rows, width), BF16)
    return call(
        prepare_body,
        [IN_HBM] * 5,
        [
            wide,
            wide,
            shaped((rows, LANES), BF16),
            shaped((blocks * ROWS, width), F32),
            shaped(layer_input.shape, BF16),
        ],
        "prepare",
        [wide, wide, shaped(keep.shape, BF16), shaped(step.shape, BF16), pltpu.SemaphoreType.DMA((2 * blocks + 3,))],
    )(at, *in_hbm(y_grad, x_in, keep, step, layer_input))


def in_gram_body(at_ref, layer_ref, in_x, in_y, in_kx, in_ky, gram_ref):
    width = layer_ref.shape[1]
    part, half = width // 4, width // 2
    gram_ref[...] = dot(layer_ref[...], layer_ref[...], 0, 0).astype(BF16)
    places = ((1, in_x, 0, in_ky, 1), (3, in_x, 1, in_y, 1), (2, in_kx, 1, in_y, 0), (0, in_kx, 0, in_ky, 0))
    for flip, left, left_at, right, right_at in places:
        start = pl.multiple_of((at_ref[SEQ] ^ flip) * part, part)
        rows_of = gram_ref[pl.ds(start, part), :]
        left[left_at * part : (left_at + 1) * part] = rows_of[:, :half]
        right[right_at * part : (right_at + 1) * part] = rows_of[:, half:]


def in_gram(at, layer_input):
    cols = layer_input.shape[1]
    return call(
        in_gram_body,
        [IN_VMEM],
        [shaped((cols // 2, cols // 2), BF16)] * 4,
        "in_gram",
        [shaped((cols, cols), BF16)],
    )(at, layer_input)


def block_rows(at_ref, mine_ref, other_ref, block, side=None):
    swap = at_ref[CORE] == 1
    place = at_ref[PLACE + block]
    state = mine_ref.shape[2] // 2
    cols = slice(None) if side is None else slice(side * state, (side + 1) * state)
    mine, other = mine_ref[place][:, cols], other_ref[place][:, cols]
    return jnp.concatenate([jnp.where(swap, other, mine), jnp.where(swap, mine, other)], axis=0)


def state_body(at_ref, mine_ref, other_ref, gu_ref, xv_ref, decay_ref, back_ref, front_ref, *sent_refs):
    state = mine_ref.shape[2] // 2
    blocks = gu_ref.shape[0] // SPAN
    totals = []
    for val_ref, own_ref, side in ((gu_ref, back_ref, 1), (xv_ref, front_ref, 0)):
        carry = mine = None
        for block in reversed(range(blocks)) if side else range(blocks):
            rows = block_rows(at_ref, mine_ref, other_ref, block, side)
            at = block * ROWS
            own = dot(rows, val_ref[block * SPAN : (block + 1) * SPAN], 0, 0)
            own = own * decay_ref[at + 1 - side : at + 2 - side]
            own_ref[block * state : (block + 1) * state] = own
            decay = decay_ref[at + 2 : at + 3]
            carry = own if carry is None else carry * decay + own
            mine = decay if mine is None else mine * decay
        totals.append(carry)
    back, front = totals
    if len(sent_refs) == 2:
        sent_refs[0][...] = back.astype(BF16)
        sent_refs[1][...] = front.astype(BF16)
        return
    high = mine.astype(BF16).astype(F32)
    row = iota((NOTE, mine.shape[1]), 0)
    note = jnp.where(row == 0, high, jnp.where(row == 1, mine - high, 0.0)).astype(BF16)
    back, front = back.astype(BF16), front.astype(BF16)
    for flip, ref in zip((3, 2, 1), sent_refs):
        to_earlier = (at_ref[SEQ] ^ flip) < at_ref[SEQ]
        ref[:state] = jnp.where(to_earlier, back, front)
        ref[state:] = note


def device_states(at, gathered, gu, xv, decays, square):
    rows, width = gu.shape
    state = gathered[0].shape[2] // 2
    own = shaped((rows // SPAN * state, width), F32)
    total = shaped((state, width), BF16)
    sent = [shaped((state + NOTE, width), BF16)] * 3 if square else [total, total]
    return call(state_body, [IN_VMEM] * 5, [own, own] + sent, "states")(at, *gathered, gu, xv, decays)


def enter(at_ref, refs, state, backward):
    notes = [ref[state:].astype(F32) for ref in refs]
    near_d, near_y, near_x = [note[0:1] + note[1:2] for note in notes]
    diagonal, along_y, along_x = [ref[:state].astype(F32) for ref in refs]
    one, zero = jnp.ones_like(near_x), jnp.zeros_like(near_x)
    place = at_ref[SEQ] if backward else 3 - at_ref[SEQ]

    def choose(*rows):
        picked = zero
        for at, row in enumerate(rows):
            picked = jnp.where(place == at, row, picked)
        return picked

    return (
        along_x * choose(one, zero, one, zero)
        + along_y * choose(near_x, near_d, zero, zero)
        + diagonal * choose(near_x * near_y, one, zero, zero)
    )


def local_body(
    at_ref, mine_ref, other_ref, val_ref, packed_ref, decay_ref, own_ref, out_ref, factor_ref, scale_ref, *, backward
):
    width = val_ref.shape[1]
    state = mine_ref.shape[2] // 2
    blocks = val_ref.shape[0] // SPAN
    pick = 1 if backward else 0
    taken = spread(width // HEAD_DIM, width, 2 if backward else 0)
    down, across = iota((SPAN, SPAN), 0), iota((SPAN, SPAN), 1)
    keep = down <= across if backward else down >= across
    entering = jnp.zeros((state, width), F32)
    left = jnp.ones((1, width), F32)
    scale_ref[...] = jnp.zeros_like(scale_ref)
    for block in reversed(range(blocks)) if backward else range(blocks):
        cut = slice(block * SPAN, (block + 1) * SPAN)
        at = block * ROWS
        proj = block_rows(at_ref, mine_ref, other_ref, block)
        b_rows, c_rows = proj[:, :state], proj[:, state:]
        rows_of, cols_of = (b_rows, c_rows) if backward else (c_rows, b_rows)
        score = jnp.where(keep, dot(rows_of, cols_of, 1, 1), 0.0).astype(BF16)
        scale = decay_ref[at + pick : at + pick + 1]
        total = dot(score, val_ref[cut]) + dot(rows_of, (entering * scale).astype(BF16))
        factor = dot(packed_ref[cut], taken)
        factor_ref[cut] = factor
        out_ref[cut] = total * factor
        scale_ref[block : block + 1] = scale * left
        decay = decay_ref[at + 2 : at + 3]
        entering = entering * decay + own_ref[block * state : (block + 1) * state]
        left = left * decay


def local_outputs(at, gathered, values, packed, decays, own, backward):
    rows, width = values.shape
    wide = shaped((rows, width), F32)
    return call(
        functools.partial(local_body, backward=backward),
        [IN_VMEM] * 6,
        [wide, wide, shaped((ROWS, width), F32)],
        "local_back" if backward else "local_front",
        mib=32,
    )(at, *gathered, values, packed, decays, own)


def outputs_body(at_ref, mine_ref, other_ref, local_ref, factor_ref, scale_ref, *rest, backward, square):
    got_count = 3 if square else 2
    got_refs, out_hbm, (kept, *gram_refs), left = rest[:got_count], rest[got_count], rest[got_count + 1 : -1], rest[-1]
    state = mine_ref.shape[2] // 2
    blocks = local_ref.shape[0] // SPAN
    if square:
        entering = enter(at_ref, got_refs, state, backward)
    else:
        entering = got_refs[0][...].astype(F32) + got_refs[1][...].astype(F32)
    moves = []
    for block in range(blocks):
        cut = slice(block * SPAN, (block + 1) * SPAN)
        rows_of = block_rows(at_ref, mine_ref, other_ref, block, 0 if backward else 1)
        far = dot(rows_of, (entering * scale_ref[block : block + 1]).astype(BF16))
        kept[cut] = (local_ref[cut] + far * factor_ref[cut]).astype(BF16)
        rows = pl.ds(block * SPAN, SPAN)
        moves.append(pltpu.make_async_copy(kept.at[rows, :], out_hbm.at[rows, :], left.at[block]))
        moves[-1].start()
    if gram_refs:
        first_messages(at_ref, kept, *gram_refs)
    for move in moves:
        move.wait()


def gram_row(at_ref, rows_ref, flip):
    part = rows_ref.shape[1] // 4
    cols = lambda turned: pl.ds(pl.multiple_of((at_ref[SEQ] ^ turned) * part, part), part)
    turned_rows = rows_ref[:, cols(flip)].T
    return lambda col: dot(turned_rows, rows_ref[:, cols(col)]).astype(BF16)


def first_messages(at_ref, rows_ref, x_ref, y_ref):
    part = rows_ref.shape[1] // 4
    half = part // 2
    block = gram_row(at_ref, rows_ref, 3)
    on_c, on_own = block(3), block(0)
    for ref, cut, pair in ((x_ref, slice(0, half), 1), (y_ref, slice(half, part), 2)):
        ref[:, :half] = on_c[:, cut]
        ref[:, half:part] = on_own[:, cut]
        ref[:, part:] = block(pair)


def outputs(at, gathered, local, got, backward, square=True):
    rows, width = local[0].shape
    out_shape = [pltpu.HBM((rows, width), BF16)]
    scratch = [pltpu.SemaphoreType.DMA((rows // SPAN,))]
    if backward and square:
        out_shape += [shaped((rows, width), BF16)] + [shaped((width // 4, width // 2), BF16)] * 2
    else:
        scratch = [pltpu.VMEM((rows, width), BF16)] + scratch
    return call(
        functools.partial(outputs_body, backward=backward, square=square),
        [IN_VMEM] * (5 + len(got)),
        out_shape,
        "back_outputs" if backward else "front_outputs",
        scratch,
        [IN_HBM] + [IN_VMEM] * (len(out_shape) - 1),
    )(at, *gathered, *local, *got)


def rest_body(at_ref, rows_ref, in_kx, in_x1, in_ky, in_y1, x_ref, y_ref, kept_x, kept_y, own_ref):
    part = rows_ref.shape[1] // 4
    half = part // 2
    in_part = in_kx.shape[0] // 2
    for kept, got, out in ((in_kx, in_x1, y_ref), (in_ky, in_y1, x_ref)):
        out[part:] = (kept[in_part:].astype(F32) + got[in_part:].astype(F32)).astype(BF16)
    low, high = slice(0, half), slice(half, part)
    for flip, other, sent, kept, now, later in ((1, 2, x_ref, kept_x, low, high), (2, 1, y_ref, kept_y, high, low)):
        block = gram_row(at_ref, rows_ref, flip)
        on_self, on_other = block(flip), block(other)
        sent[:part, :half] = on_self[:, now]
        sent[:part, half:] = on_other[:, now]
        kept[:, :half] = on_self[:, later]
        kept[:, half:part] = on_other[:, later]
        kept[:, part:] = block(0)
    block = gram_row(at_ref, rows_ref, 0)
    own_ref[:, :part] = block(0)
    own_ref[:, part:] = block(3)


def rest_gram(at, x_grad, in_parts):
    width = x_grad.shape[1]
    part = width // 4
    sent = shaped((part + in_parts[0].shape[0] // 2, part), BF16)
    kept = shaped((part, width // 2), BF16)
    return call(
        rest_body,
        [IN_VMEM] * 5,
        [sent, sent, kept, kept, kept],
        "rest_gram",
    )(at, x_grad, *in_parts)


def middle_body(at_ref, own_ref, x2_ref, y2_ref, x3_ref, y3_ref, out_ref):
    part = own_ref.shape[0]
    half = part // 2
    for at in range(2):
        start = at * part
        cut = slice(at * half, (at + 1) * half)
        for side, ref in enumerate((x2_ref, y2_ref)):
            cols = slice(start + side * half, start + (side + 1) * half)
            out_ref[:, cols] = own_ref[:, cols].astype(F32) + ref[:part, cut].astype(F32)
    for at, ref in ((2, x3_ref), (3, y3_ref)):
        out_ref[:, at * part : (at + 1) * part] = ref[:, part:].astype(F32).T


def middle(at, own, x2, y2, x3, y3):
    rows, width = own.shape
    return call(middle_body, [IN_VMEM] * 5, [shaped((rows, 2 * width), F32)], "middle")(
        at, own, x2, y2, x3, y3
    )[0]


def last_body(at_ref, base_ref, x_ref, y_ref, out_hbm, out_ref, left, *, scale):
    rows, width = out_ref.shape
    part = width // 4
    half = part // 2
    moves = []
    for piece in range(PIECES):
        cut = slice(piece * rows // PIECES, (piece + 1) * rows // PIECES)
        for at, flip in enumerate((0, 3, 1, 2)):
            cols = slice(at * half, (at + 1) * half)
            if flip in (0, 3):
                got = jnp.concatenate([y_ref[cut, cols], x_ref[cut, cols]], axis=1)
            else:
                got = (x_ref if flip == 1 else y_ref)[cut, part:]
            start = pl.multiple_of((at_ref[SEQ] ^ flip) * part, part)
            total = base_ref[cut, at * part : (at + 1) * part] + got.astype(F32)
            out_ref[cut, pl.ds(start, part)] = total * scale
        some = pl.ds(piece * rows // PIECES, rows // PIECES)
        moves.append(pltpu.make_async_copy(out_ref.at[some, :], out_hbm.at[some, :], left.at[piece]))
        moves[-1].start()
    for move in moves:
        move.wait()


def last(at, base, x_got, y_got, seq_total):
    return call(
        functools.partial(last_body, scale=1.0 / seq_total),
        [IN_VMEM] * 3,
        [pltpu.HBM(base.shape, F32)],
        "finish_grad",
        [pltpu.VMEM(base.shape, F32), pltpu.SemaphoreType.DMA((PIECES,))],
        [IN_HBM],
    )(at, base, x_got, y_got)[0]


def finish_body(at_ref, *refs, scale):
    parts, (out_hbm, out_ref, left) = refs[:6], refs[6:]
    rows, width = out_ref.shape
    half = width // 2
    moves = []
    for side in range(2):
        one, two, three = parts[3 * side : 3 * side + 3]
        last = three[...]
        cols = pl.ds(side * half, half)
        out_ref[:, cols] = (one[:rows].astype(F32) + two[:rows].astype(F32) + last.astype(F32)) * scale
        moves.append(pltpu.make_async_copy(out_ref.at[:, cols], out_hbm.at[:, cols], left.at[side]))
        moves[-1].start()
    for move in moves:
        move.wait()


def finish(at, left, right, shape, seq_total, name):
    return call(
        functools.partial(finish_body, scale=1.0 / seq_total),
        [IN_VMEM] * 6,
        [pltpu.HBM(shape, F32)],
        name,
        [pltpu.VMEM(shape, F32), pltpu.SemaphoreType.DMA((2,))],
        [IN_HBM],
    )(at, *left, *right)[0]


def after(value, *others):
    return lax.optimization_barrier((value, *others))[0]


def gather_rows(rows_in, *others):
    mp_count = lax.axis_size("mp")
    pieces = [rows_in]
    for shift in range(1, mp_count // 2):
        perm = [(m, (m + 2 * shift) % mp_count) for m in range(mp_count)]
        pieces.append(lax.ppermute(rows_in, "mp", perm))
    mine = after(jnp.stack(pieces), *others)
    return mine, lax.ppermute(mine, "mp", [(m, m ^ 1) for m in range(mp_count)])


def order_rows(mine, other):
    z_count, count, width = mine.shape
    z_at, core = lax.axis_index("mp") // 2, lax.axis_index("mp") % 2
    order = (z_at - jnp.arange(z_count)) % z_count
    pair = jnp.where(core == 0, jnp.stack([mine, other], axis=1), jnp.stack([other, mine], axis=1))
    rows = pair[order].reshape(-1, 2, SPAN // 2, width)
    return rows[:, 0], rows[:, 1]


X_PAIRS = [(0, 1), (1, 0), (2, 3), (3, 2)]
Y_PAIRS = [(0, 2), (2, 0), (1, 3), (3, 1)]
D_PAIRS = [(0, 3), (3, 0), (1, 2), (2, 1)]


def go(value, pairs):
    return lax.ppermute(value, "seq", pairs)


def added(one, two):
    return (one.astype(F32) + two.astype(F32)).astype(BF16)


def square_shards(x_in, step_size, log_keep, b_proj, c_proj, y_grad, layer_input):
    tok_rows, width = x_in.shape
    seq_total = tok_rows * 4
    z_count = lax.axis_size("mp") // 2
    z_at, core = lax.axis_index("mp") // 2, lax.axis_index("mp") % 2
    direct = b_proj.shape[0] * 2 == SPAN
    places = jnp.arange(tok_rows // SPAN)
    if direct:
        places = (z_at - places) % z_count
    at = jnp.concatenate([jnp.stack([lax.axis_index("seq"), core if direct else 0]), places])
    at = at.astype(jnp.int32)

    joined = join(at, b_proj, c_proj)
    gu, xv, packed, decays, layer = prepare(at, y_grad, x_in, log_keep.T, step_size.T, layer_input)
    gathered = gather_rows(joined, decays)
    if not direct:
        gathered = order_rows(*gathered)

    own_back, own_front, diagonal, along_y, along_x = device_states(at, gathered, gu, xv, decays, True)
    along_x, along_y, diagonal = go(along_x, X_PAIRS), go(along_y, Y_PAIRS), go(diagonal, D_PAIRS)
    got = (diagonal, along_y, along_x)
    local_back = local_outputs(at, gathered, gu, packed, decays, own_back, True)
    local_front = local_outputs(at, gathered, xv, packed, decays, own_front, False)
    in_x, in_y, in_kx, in_ky = in_gram(at, after(layer, diagonal, local_back[2], local_front[2]))
    in_x1, in_y1 = go(in_x, X_PAIRS), go(in_y, Y_PAIRS)
    x_grad, kept, x_first, y_first = outputs(at, gathered, local_back, got, True)

    x_first_in, y_first_in = go(x_first, X_PAIRS), go(y_first, Y_PAIRS)
    x_second, y_second, kept_x, kept_y, gram_own = rest_gram(at, kept, (in_kx, in_x1, in_ky, in_y1))
    x_second_in, y_second_in = go(x_second, X_PAIRS), go(y_second, Y_PAIRS)
    y_third, x_third = added(x_first_in, kept_y), added(y_first_in, kept_x)
    y_third_in, x_third_in = go(y_third, Y_PAIRS), go(x_third, X_PAIRS)
    y_out = outputs(at, gathered, local_front, got, False)[0]
    in_part = layer_input.shape[1] // 4
    in_factor = finish(
        at,
        (in_kx, in_x1, y_second_in[width // 4 :]),
        (in_ky, in_y1, x_second_in[width // 4 :]),
        (in_part, 4 * in_part),
        seq_total,
        "finish_in",
    )
    base = middle(at, gram_own, x_second_in, y_second_in, x_third, y_third)
    grad_factor = last(at, base, x_third_in, y_third_in, seq_total)
    return (y_out, x_grad, in_factor, grad_factor)


def enter_any(total, decay_all, seq_at, backward):
    seq_count = decay_all.shape[0]
    totals = lax.all_gather(total, "seq")
    if not backward:
        totals, decay_all, seq_at = totals[::-1], decay_all[::-1], seq_count - 1 - seq_at
    entering = jnp.zeros(total.shape, F32)
    for at in range(seq_count - 1, 0, -1):
        moved = jnp.repeat(decay_all[at], HEAD_DIM) * entering + totals[at].astype(F32)
        entering = jnp.where(at > seq_at, moved, entering)
    high = entering.astype(BF16)
    low = (entering - high.astype(F32)).astype(BF16)
    return high, low


def summed(rows, seq_total):
    gram = dot(rows, rows, 0, 0).astype(BF16)
    total = lax.psum_scatter(gram, "seq", scatter_dimension=0, tiled=True)
    return total.astype(F32) / seq_total


def any_shards(x_in, step_size, log_keep, b_proj, c_proj, y_grad, layer_input):
    tok_rows, width = x_in.shape
    heads = step_size.shape[1]
    seq_total = tok_rows * lax.axis_size("seq")
    seq_at = lax.axis_index("seq")
    at = jnp.concatenate([jnp.zeros((2,), jnp.int32), jnp.arange(tok_rows // SPAN, dtype=jnp.int32)])
    decay_all = lax.all_gather(jnp.exp(jnp.sum(log_keep.astype(F32), axis=0)), "seq")
    joined = join(at, b_proj, c_proj)
    gathered = order_rows(*gather_rows(joined))
    gu, xv, packed, decays, layer = prepare(at, y_grad, x_in, log_keep.T, step_size.T, layer_input)
    own_back, own_front, back, front = device_states(at, gathered, gu, xv, decays, False)
    results = []
    for values, own, total, backward in ((gu, own_back, back, True), (xv, own_front, front, False)):
        got = enter_any(total, decay_all, seq_at, backward)
        local = local_outputs(at, gathered, values, packed, decays, own, backward)
        results.append(outputs(at, gathered, local, got, backward, False)[0])
    x_grad, y_out = results
    return (y_out, x_grad, summed(layer, seq_total), summed(x_grad, seq_total))


def solution(mesh):
    spec = P("seq", "mp")
    rows = P(("seq", "mp"), None)
    return jax.shard_map(
        square_shards if mesh.shape["seq"] == 4 else any_shards,
        mesh=mesh,
        in_specs=(spec, spec, spec, rows, rows, spec, spec),
        out_specs=(spec, spec, spec, spec),
        check_vma=False,
    )
```

```python
import functools

import jax
import jax.numpy as jnp
import numpy as np
from jax import lax
from jax.experimental import pallas as pl
from jax.experimental.pallas import tpu as pltpu
from jax.sharding import PartitionSpec as P

HEAD_DIM = 64
SPAN = 256
F32 = jnp.float32
BF16 = jnp.bfloat16
ROWS = 8
LANES = 128
NOTE = 8
PIECES = 4
SEQ, CORE, PLACE = 0, 1, 2


def iota(shape, axis):
    return lax.broadcasted_iota(jnp.int32, shape, axis)


IN_HBM = pl.BlockSpec(memory_space=pltpu.HBM)
IN_SMEM = pl.BlockSpec(memory_space=pltpu.SMEM)
IN_VMEM = pl.BlockSpec(memory_space=pltpu.VMEM)


def shaped(shape, dtype):
    return pltpu.VMEM(shape, dtype)


def in_hbm(*arrays):
    return [pltpu.with_memory_space_constraint(array, pltpu.HBM) for array in arrays]


TAKES = {
    "join_projections": 1.7,
    "prepare": 5.5,
    "in_gram": 1.3,
    "second_in": 0.6,
    "states": 2.2,
    "local_back": 3.0,
    "local_front": 3.0,
    "back_outputs": 2.5,
    "front_outputs": 0.01,
    "rest_gram": 2.4,
    "finish_in": 0.01,
    "middle": 0.01,
    "finish_grad": 1.6,
}


def in_vmem(*arrays):
    return [pltpu.with_memory_space_constraint(array, pltpu.VMEM) for array in arrays]


def call(body, in_specs, out_shape, name, scratch=(), out_specs=None, mib=24):
    takes = TAKES[name]
    cost = pl.CostEstimate(
        flops=int(takes * 1.15e9), bytes_accessed=int(takes * 3.6e6), transcendentals=0
    )
    return pl.pallas_call(
        body,
        in_specs=[IN_SMEM] + in_specs,
        out_specs=out_specs or [IN_VMEM] * len(out_shape),
        out_shape=out_shape,
        scratch_shapes=list(scratch),
        compiler_params=pltpu.CompilerParams(vmem_limit_bytes=mib << 20),
        cost_estimate=cost,
        name=name,
    )


def dot(left, right, left_axis=1, right_axis=0):
    return lax.dot_general(
        left, right, (((left_axis,), (right_axis,)), ((), ())), preferred_element_type=F32
    )


def bits(count):
    if count & (count - 1):
        raise ValueError("power of 2")
    return count.bit_length() - 1


def spread(heads, width, first):
    lane = iota((LANES, width), 0)
    hit = (lane & (heads - 1)) == (iota((LANES, width), 1) >> bits(HEAD_DIM))
    group = lane >> bits(heads)
    return (hit & ((group >> 1) == first // 2)).astype(F32).astype(BF16)


def copies(heads):
    lane = iota((heads, LANES), 1)
    hit = ((lane & (heads - 1)) == iota((heads, LANES), 0)) & (lane < 4 * heads)
    return hit.astype(F32).astype(BF16)


def split_parts(values, heads):
    high = values.astype(BF16)
    low = (values - high.astype(F32)).astype(BF16)
    is_low = ((iota(values.shape, 1) >> bits(heads)) & 1) == 1
    return jnp.where(is_low, low.astype(F32), high.astype(F32)).astype(BF16)


def join_body(at_ref, b_hbm, c_hbm, out_ref, arrived):
    state = b_hbm.shape[1]
    moves = [
        pltpu.make_async_copy(b_hbm, out_ref.at[:, pl.ds(0, state)], arrived.at[0]),
        pltpu.make_async_copy(c_hbm, out_ref.at[:, pl.ds(state, state)], arrived.at[1]),
    ]
    for move in moves:
        move.start()
    for move in moves:
        move.wait()


def join(at, b_proj, c_proj):
    rows, state = b_proj.shape
    return call(
        join_body,
        [IN_HBM] * 2,
        [shaped((rows, 2 * state), BF16)],
        "join_projections",
        [pltpu.SemaphoreType.DMA((2,))],
    )(at, *in_hbm(b_proj, c_proj))[0]


def prepare_body(at_ref, g_ref, x_ref, keep_ref, step_ref, gu_ref, xv_ref, packed_ref, decay_ref):
    rows, width = g_ref.shape
    heads = keep_ref.shape[0]
    blocks = rows // SPAN
    cuts = [slice(block * SPAN, (block + 1) * SPAN) for block in range(blocks)]
    lower = (iota((SPAN, SPAN), 0) >= iota((SPAN, SPAN), 1)).astype(F32).astype(BF16)
    take_u, take_v, copied = spread(heads, width, 0), spread(heads, width, 2), copies(heads)
    keep = dot(keep_ref[...], copied, 0, 0).astype(BF16)
    step = dot(step_ref[...], copied, 0, 0)
    cums = [dot(lower, keep[cut]) for cut in cuts]
    mids = [cum[SPAN // 2 - 1 : SPAN // 2] for cum in cums]
    ends = [cum[SPAN - 1 : SPAN] for cum in cums]
    offset = jnp.concatenate([cum - mid for cum, mid in zip(cums, mids)], axis=0)
    on_u = (iota((rows, LANES), 1) >> bits(heads)) < 2
    factor = jnp.exp(jnp.where(on_u, offset, -offset)) * jnp.where(on_u, 1.0, step)
    packed_ref[...] = split_parts(factor, heads)
    row = iota((ROWS, LANES), 0)
    logs = [jnp.where(row == 0, mid, jnp.where(row == 1, end - mid, end)) for mid, end in zip(mids, ends)]
    decay_ref[...] = dot(split_parts(jnp.exp(jnp.concatenate(logs, axis=0)), heads), take_u)
    for ref, taken, out_ref in ((g_ref, take_u, gu_ref), (x_ref, take_v, xv_ref)):
        for cut in cuts:
            out_ref[cut] = (ref[cut].astype(F32) * dot(packed_ref[cut], taken)).astype(BF16)


def prepare(at, y_grad, x_in, keep, step):
    rows, width = x_in.shape
    blocks = rows // SPAN
    wide = shaped((rows, width), BF16)
    return call(
        prepare_body,
        [IN_VMEM] * 4,
        [wide, wide, shaped((rows, LANES), BF16), shaped((blocks * ROWS, width), F32)],
        "prepare",
    )(at, *in_vmem(y_grad, x_in, keep, step))


def in_gram_body(at_ref, layer_ref, in_x, in_y, in_kx, in_ky, gram_ref):
    width = layer_ref.shape[1]
    part, half = width // 4, width // 2
    gram_ref[...] = dot(layer_ref[...], layer_ref[...], 0, 0).astype(BF16)
    places = ((1, in_x, 0, in_ky, 1), (3, in_x, 1, in_y, 1), (2, in_kx, 1, in_y, 0), (0, in_kx, 0, in_ky, 0))
    for flip, left, left_at, right, right_at in places:
        start = pl.multiple_of((at_ref[SEQ] ^ flip) * part, part)
        rows_of = gram_ref[pl.ds(start, part), :]
        left[left_at * part : (left_at + 1) * part] = rows_of[:, :half]
        right[right_at * part : (right_at + 1) * part] = rows_of[:, half:]


def in_gram(at, layer_input):
    cols = layer_input.shape[1]
    return call(
        in_gram_body,
        [IN_VMEM],
        [shaped((cols // 2, cols // 2), BF16)] * 4,
        "in_gram",
        [shaped((cols, cols), BF16)],
    )(at, *in_vmem(layer_input))


def block_rows(at_ref, mine_ref, other_ref, block, side=None):
    swap = at_ref[CORE] == 1
    place = at_ref[PLACE + block]
    state = mine_ref.shape[2] // 2
    cols = slice(None) if side is None else slice(side * state, (side + 1) * state)
    mine, other = mine_ref[place][:, cols], other_ref[place][:, cols]
    return jnp.concatenate([jnp.where(swap, other, mine), jnp.where(swap, mine, other)], axis=0)


def state_body(at_ref, mine_ref, other_ref, gu_ref, xv_ref, decay_ref, back_ref, front_ref, *sent_refs):
    state = mine_ref.shape[2] // 2
    blocks = gu_ref.shape[0] // SPAN
    totals = []
    for val_ref, own_ref, side in ((gu_ref, back_ref, 1), (xv_ref, front_ref, 0)):
        carry = mine = None
        for block in reversed(range(blocks)) if side else range(blocks):
            rows = block_rows(at_ref, mine_ref, other_ref, block, side)
            at = block * ROWS
            own = dot(rows, val_ref[block * SPAN : (block + 1) * SPAN], 0, 0)
            own = own * decay_ref[at + 1 - side : at + 2 - side]
            own_ref[block * state : (block + 1) * state] = own
            decay = decay_ref[at + 2 : at + 3]
            carry = own if carry is None else carry * decay + own
            mine = decay if mine is None else mine * decay
        totals.append(carry)
    back, front = totals
    if len(sent_refs) == 2:
        sent_refs[0][...] = back.astype(BF16)
        sent_refs[1][...] = front.astype(BF16)
        return
    high = mine.astype(BF16).astype(F32)
    row = iota((NOTE, mine.shape[1]), 0)
    note = jnp.where(row == 0, high, jnp.where(row == 1, mine - high, 0.0)).astype(BF16)
    back, front = back.astype(BF16), front.astype(BF16)
    for flip, ref in zip((1, 2, 3), sent_refs):
        to_earlier = (at_ref[SEQ] ^ flip) < at_ref[SEQ]
        ref[:state] = jnp.where(to_earlier, back, front)
        ref[state:] = note


def device_states(at, gathered, gu, xv, decays, square):
    rows, width = gu.shape
    state = gathered[0].shape[2] // 2
    own = shaped((rows // SPAN * state, width), F32)
    total = shaped((state, width), BF16)
    sent = [shaped((state + NOTE, width), BF16)] * 3 if square else [total, total]
    return call(state_body, [IN_VMEM] * 5, [own, own] + sent, "states")(at, *gathered, gu, xv, decays)


def enter(at_ref, refs, state, backward):
    notes = [ref[state:].astype(F32) for ref in refs]
    near_x, near_y, near_d = [note[0:1] + note[1:2] for note in notes]
    along_x, along_y, diagonal = [ref[:state].astype(F32) for ref in refs]
    one, zero = jnp.ones_like(near_x), jnp.zeros_like(near_x)
    place = at_ref[SEQ] if backward else 3 - at_ref[SEQ]

    def choose(*rows):
        picked = zero
        for at, row in enumerate(rows):
            picked = jnp.where(place == at, row, picked)
        return picked

    return (
        along_x * choose(one, zero, one, zero)
        + along_y * choose(near_x, near_d, zero, zero)
        + diagonal * choose(near_x * near_y, one, zero, zero)
    )


def local_body(
    at_ref, mine_ref, other_ref, val_ref, packed_ref, decay_ref, own_ref, out_ref, factor_ref, scale_ref, *, backward
):
    width = val_ref.shape[1]
    state = mine_ref.shape[2] // 2
    blocks = val_ref.shape[0] // SPAN
    pick = 1 if backward else 0
    taken = spread(width // HEAD_DIM, width, 2 if backward else 0)
    down, across = iota((SPAN, SPAN), 0), iota((SPAN, SPAN), 1)
    keep = down <= across if backward else down >= across
    entering = jnp.zeros((state, width), F32)
    left = jnp.ones((1, width), F32)
    scale_ref[...] = jnp.zeros_like(scale_ref)
    for block in reversed(range(blocks)) if backward else range(blocks):
        cut = slice(block * SPAN, (block + 1) * SPAN)
        at = block * ROWS
        proj = block_rows(at_ref, mine_ref, other_ref, block)
        b_rows, c_rows = proj[:, :state], proj[:, state:]
        rows_of, cols_of = (b_rows, c_rows) if backward else (c_rows, b_rows)
        score = jnp.where(keep, dot(rows_of, cols_of, 1, 1), 0.0).astype(BF16)
        scale = decay_ref[at + pick : at + pick + 1]
        total = dot(score, val_ref[cut]) + dot(rows_of, (entering * scale).astype(BF16))
        factor = dot(packed_ref[cut], taken)
        factor_ref[cut] = factor
        out_ref[cut] = total * factor
        scale_ref[block : block + 1] = scale * left
        decay = decay_ref[at + 2 : at + 3]
        entering = entering * decay + own_ref[block * state : (block + 1) * state]
        left = left * decay


def local_outputs(at, gathered, values, packed, decays, own, backward):
    rows, width = values.shape
    wide = shaped((rows, width), F32)
    return call(
        functools.partial(local_body, backward=backward),
        [IN_VMEM] * 6,
        [wide, wide, shaped((ROWS, width), F32)],
        "local_back" if backward else "local_front",
        mib=32,
    )(at, *gathered, values, packed, decays, own)


def outputs_body(at_ref, mine_ref, other_ref, local_ref, factor_ref, scale_ref, *rest, backward, square):
    got_count = 3 if square else 2
    got_refs, out_hbm, (kept, *gram_refs), left = rest[:got_count], rest[got_count], rest[got_count + 1 : -1], rest[-1]
    state = mine_ref.shape[2] // 2
    blocks = local_ref.shape[0] // SPAN
    if square:
        entering = enter(at_ref, got_refs, state, backward)
    else:
        entering = got_refs[0][...].astype(F32) + got_refs[1][...].astype(F32)
    moves = []
    for block in range(blocks):
        cut = slice(block * SPAN, (block + 1) * SPAN)
        rows_of = block_rows(at_ref, mine_ref, other_ref, block, 0 if backward else 1)
        far = dot(rows_of, (entering * scale_ref[block : block + 1]).astype(BF16))
        kept[cut] = (local_ref[cut] + far * factor_ref[cut]).astype(BF16)
        rows = pl.ds(block * SPAN, SPAN)
        moves.append(pltpu.make_async_copy(kept.at[rows, :], out_hbm.at[rows, :], left.at[block]))
        moves[-1].start()
    if gram_refs:
        first_messages(at_ref, kept, *gram_refs)
    for move in moves:
        move.wait()


def gram_row(at_ref, rows_ref, flip):
    part = rows_ref.shape[1] // 4
    cols = lambda turned: pl.ds(pl.multiple_of((at_ref[SEQ] ^ turned) * part, part), part)
    turned_rows = rows_ref[:, cols(flip)].T
    return lambda col: dot(turned_rows, rows_ref[:, cols(col)]).astype(BF16)


def first_messages(at_ref, rows_ref, x_ref, y_ref):
    part = rows_ref.shape[1] // 4
    half = part // 2
    block = gram_row(at_ref, rows_ref, 3)
    on_c, on_own = block(3), block(0)
    for ref, cut, pair in ((x_ref, slice(0, half), 1), (y_ref, slice(half, part), 2)):
        ref[:, :half] = on_c[:, cut]
        ref[:, half:part] = on_own[:, cut]
        ref[:, part:] = block(pair)


def outputs(at, gathered, local, got, backward, square=True):
    rows, width = local[0].shape
    out_shape = [pltpu.HBM((rows, width), BF16)]
    scratch = [pltpu.SemaphoreType.DMA((rows // SPAN,))]
    if backward and square:
        out_shape += [shaped((rows, width), BF16)] + [shaped((width // 4, width // 2), BF16)] * 2
    else:
        scratch = [pltpu.VMEM((rows, width), BF16)] + scratch
    return call(
        functools.partial(outputs_body, backward=backward, square=square),
        [IN_VMEM] * (5 + len(got)),
        out_shape,
        "back_outputs" if backward else "front_outputs",
        scratch,
        [IN_HBM] + [IN_VMEM] * (len(out_shape) - 1),
    )(at, *gathered, *local, *got)


def second_body(at_ref, in_kx, in_x1, in_ky, in_y1, x_ref, y_ref):
    part = in_kx.shape[0] // 2
    for kept, got, out in ((in_kx, in_x1, x_ref), (in_ky, in_y1, y_ref)):
        out[...] = (kept[part:].astype(F32) + got[part:].astype(F32)).astype(BF16)


def second_in(at, in_kx, in_x1, in_ky, in_y1):
    part = shaped((in_kx.shape[0] // 2, in_kx.shape[1]), BF16)
    return call(second_body, [IN_VMEM] * 4, [part, part], "second_in")(at, in_kx, in_x1, in_ky, in_y1)


def rest_body(at_ref, rows_ref, x_ref, y_ref, kept_x, kept_y, own_ref):
    part = rows_ref.shape[1] // 4
    half = part // 2
    low, high = slice(0, half), slice(half, part)
    for flip, other, sent, kept, now, later in ((1, 2, x_ref, kept_x, low, high), (2, 1, y_ref, kept_y, high, low)):
        block = gram_row(at_ref, rows_ref, flip)
        on_self, on_other = block(flip), block(other)
        sent[:, :half] = on_self[:, now]
        sent[:, half:] = on_other[:, now]
        kept[:, :half] = on_self[:, later]
        kept[:, half:part] = on_other[:, later]
        kept[:, part:] = block(0)
    block = gram_row(at_ref, rows_ref, 0)
    own_ref[:, :part] = block(0)
    own_ref[:, part:] = block(3)


def rest_gram(at, x_grad):
    width = x_grad.shape[1]
    part = width // 4
    sent, kept = shaped((part, part), BF16), shaped((part, width // 2), BF16)
    return call(rest_body, [IN_VMEM], [sent, sent, kept, kept, kept], "rest_gram")(at, x_grad)


def middle_body(at_ref, own_ref, x2_ref, y2_ref, x3_ref, y3_ref, out_ref):
    part = own_ref.shape[0]
    half = part // 2
    for at in range(2):
        start = at * part
        cut = slice(at * half, (at + 1) * half)
        for side, ref in enumerate((x2_ref, y2_ref)):
            cols = slice(start + side * half, start + (side + 1) * half)
            out_ref[:, cols] = own_ref[:, cols].astype(F32) + ref[:part, cut].astype(F32)
    for at, ref in ((2, x3_ref), (3, y3_ref)):
        out_ref[:, at * part : (at + 1) * part] = ref[:, part:].astype(F32).T


def middle(at, own, x2, y2, x3, y3):
    rows, width = own.shape
    return call(middle_body, [IN_VMEM] * 5, [shaped((rows, 2 * width), F32)], "middle")(
        at, own, x2, y2, x3, y3
    )[0]


def last_body(at_ref, base_ref, x_ref, y_ref, out_hbm, out_ref, left, *, scale):
    rows, width = out_ref.shape
    part = width // 4
    half = part // 2
    moves = []
    for piece in range(PIECES):
        cut = slice(piece * rows // PIECES, (piece + 1) * rows // PIECES)
        for at, flip in enumerate((0, 3, 1, 2)):
            cols = slice(at * half, (at + 1) * half)
            if flip in (0, 3):
                got = jnp.concatenate([y_ref[cut, cols], x_ref[cut, cols]], axis=1)
            else:
                got = (x_ref if flip == 1 else y_ref)[cut, part:]
            start = pl.multiple_of((at_ref[SEQ] ^ flip) * part, part)
            total = base_ref[cut, at * part : (at + 1) * part] + got.astype(F32)
            out_ref[cut, pl.ds(start, part)] = total * scale
        some = pl.ds(piece * rows // PIECES, rows // PIECES)
        moves.append(pltpu.make_async_copy(out_ref.at[some, :], out_hbm.at[some, :], left.at[piece]))
        moves[-1].start()
    for move in moves:
        move.wait()


def last(at, base, x_got, y_got, seq_total):
    return call(
        functools.partial(last_body, scale=1.0 / seq_total),
        [IN_VMEM] * 3,
        [pltpu.HBM(base.shape, F32)],
        "finish_grad",
        [pltpu.VMEM(base.shape, F32), pltpu.SemaphoreType.DMA((PIECES,))],
        [IN_HBM],
    )(at, base, x_got, y_got)[0]


def finish_body(at_ref, *refs, scale):
    parts, (out_hbm, out_ref, left) = refs[:6], refs[6:]
    rows, width = out_ref.shape
    half = width // 2
    moves = []
    for side in range(2):
        one, two, three = parts[3 * side : 3 * side + 3]
        last = three[...]
        cols = pl.ds(side * half, half)
        out_ref[:, cols] = (one[:rows].astype(F32) + two[:rows].astype(F32) + last.astype(F32)) * scale
        moves.append(pltpu.make_async_copy(out_ref.at[:, cols], out_hbm.at[:, cols], left.at[side]))
        moves[-1].start()
    for move in moves:
        move.wait()


def finish(at, left, right, shape, seq_total, name):
    return call(
        functools.partial(finish_body, scale=1.0 / seq_total),
        [IN_VMEM] * 6,
        [pltpu.HBM(shape, F32)],
        name,
        [pltpu.VMEM(shape, F32), pltpu.SemaphoreType.DMA((2,))],
        [IN_HBM],
    )(at, *left, *right)[0]


def after(value, *others):
    return lax.optimization_barrier((value, *others))[0]


def gather_rows(rows_in, *others):
    mp_count = lax.axis_size("mp")
    pieces = [rows_in]
    for shift in range(1, mp_count // 2):
        perm = [(m, (m + 2 * shift) % mp_count) for m in range(mp_count)]
        pieces.append(lax.ppermute(rows_in, "mp", perm))
    mine = after(jnp.stack(pieces), *others)
    return mine, lax.ppermute(mine, "mp", [(m, m ^ 1) for m in range(mp_count)])


def order_rows(mine, other):
    z_count, count, width = mine.shape
    z_at, core = lax.axis_index("mp") // 2, lax.axis_index("mp") % 2
    order = (z_at - jnp.arange(z_count)) % z_count
    pair = jnp.where(core == 0, jnp.stack([mine, other], axis=1), jnp.stack([other, mine], axis=1))
    rows = pair[order].reshape(-1, 2, SPAN // 2, width)
    return rows[:, 0], rows[:, 1]


X_PAIRS = [(0, 1), (1, 0), (2, 3), (3, 2)]
Y_PAIRS = [(0, 2), (2, 0), (1, 3), (3, 1)]
D_PAIRS = [(0, 3), (3, 0), (1, 2), (2, 1)]


def go(value, pairs):
    return lax.ppermute(value, "seq", pairs)


def added(one, two):
    return (one.astype(F32) + two.astype(F32)).astype(BF16)


def square_shards(x_in, step_size, log_keep, b_proj, c_proj, y_grad, layer_input):
    tok_rows, width = x_in.shape
    seq_total = tok_rows * 4
    z_count = lax.axis_size("mp") // 2
    z_at, core = lax.axis_index("mp") // 2, lax.axis_index("mp") % 2
    direct = b_proj.shape[0] * 2 == SPAN
    places = jnp.arange(tok_rows // SPAN)
    if direct:
        places = (z_at - places) % z_count
    at = jnp.concatenate([jnp.stack([lax.axis_index("seq"), core if direct else 0]), places])
    at = at.astype(jnp.int32)

    joined = join(at, b_proj, c_proj)
    in_x, in_y, in_kx, in_ky = in_gram(at, layer_input)
    gu, xv, packed, decays = prepare(at, y_grad, x_in, after(log_keep.T, in_kx), step_size.T)
    gathered = gather_rows(joined, in_kx, decays)
    if not direct:
        gathered = order_rows(*gathered)

    own_back, own_front, along_x, along_y, diagonal = device_states(at, gathered, gu, xv, decays, True)
    along_x, along_y, diagonal = go(along_x, X_PAIRS), go(along_y, Y_PAIRS), go(diagonal, D_PAIRS)
    got = (along_x, along_y, diagonal)
    in_x1, in_y1 = go(in_x, X_PAIRS), go(in_y, Y_PAIRS)
    local_back = local_outputs(at, gathered, gu, packed, decays, own_back, True)
    local_front = list(local_outputs(at, gathered, xv, packed, decays, own_front, False))
    in_x2, in_y2 = second_in(at, after(in_kx, along_x, local_back[2], local_front[2]), in_x1, in_ky, in_y1)
    got = (after(along_x, in_x2), along_y, diagonal)
    in_x2, in_y2 = go(in_x2, Y_PAIRS), go(in_y2, X_PAIRS)
    x_grad, kept, x_first, y_first = outputs(at, gathered, local_back, got, True)

    x_first_in, y_first_in = go(x_first, X_PAIRS), go(y_first, Y_PAIRS)
    x_second, y_second, kept_x, kept_y, gram_own = rest_gram(at, after(kept, in_x2, in_y2))
    x_second_in, y_second_in = go(x_second, X_PAIRS), go(y_second, Y_PAIRS)
    y_third, x_third = added(x_first_in, kept_y), added(y_first_in, kept_x)
    y_third_in, x_third_in = go(y_third, Y_PAIRS), go(x_third, X_PAIRS)
    y_out = outputs(at, gathered, local_front, got, False)[0]
    in_part = layer_input.shape[1] // 4
    in_factor = finish(
        at, (in_kx, in_x1, in_x2), (in_ky, in_y1, in_y2), (in_part, 4 * in_part), seq_total, "finish_in"
    )
    base = middle(at, gram_own, x_second_in, y_second_in, x_third, y_third)
    grad_factor = last(at, base, x_third_in, y_third_in, seq_total)
    return (y_out, x_grad, in_factor, grad_factor)


def enter_any(total, decay_all, seq_at, backward):
    seq_count = decay_all.shape[0]
    totals = lax.all_gather(total, "seq")
    if not backward:
        totals, decay_all, seq_at = totals[::-1], decay_all[::-1], seq_count - 1 - seq_at
    entering = jnp.zeros(total.shape, F32)
    for at in range(seq_count - 1, 0, -1):
        moved = jnp.repeat(decay_all[at], HEAD_DIM) * entering + totals[at].astype(F32)
        entering = jnp.where(at > seq_at, moved, entering)
    high = entering.astype(BF16)
    low = (entering - high.astype(F32)).astype(BF16)
    return high, low


def summed(rows, seq_total):
    gram = dot(rows, rows, 0, 0).astype(BF16)
    total = lax.psum_scatter(gram, "seq", scatter_dimension=0, tiled=True)
    return total.astype(F32) / seq_total


def any_shards(x_in, step_size, log_keep, b_proj, c_proj, y_grad, layer_input):
    tok_rows, width = x_in.shape
    heads = step_size.shape[1]
    seq_total = tok_rows * lax.axis_size("seq")
    seq_at = lax.axis_index("seq")
    at = jnp.concatenate([jnp.zeros((2,), jnp.int32), jnp.arange(tok_rows // SPAN, dtype=jnp.int32)])
    decay_all = lax.all_gather(jnp.exp(jnp.sum(log_keep.astype(F32), axis=0)), "seq")
    joined = join(at, b_proj, c_proj)
    gathered = order_rows(*gather_rows(joined))
    gu, xv, packed, decays = prepare(at, y_grad, x_in, log_keep.T, step_size.T)
    own_back, own_front, back, front = device_states(at, gathered, gu, xv, decays, False)
    results = []
    for values, own, total, backward in ((gu, own_back, back, True), (xv, own_front, front, False)):
        got = enter_any(total, decay_all, seq_at, backward)
        local = local_outputs(at, gathered, values, packed, decays, own, backward)
        results.append(outputs(at, gathered, local, got, backward, False)[0])
    x_grad, y_out = results
    return (y_out, x_grad, summed(layer_input, seq_total), summed(x_grad, seq_total))


def solution(mesh):
    spec = P("seq", "mp")
    rows = P(("seq", "mp"), None)
    return jax.shard_map(
        square_shards if mesh.shape["seq"] == 4 else any_shards,
        mesh=mesh,
        in_specs=(spec, spec, spec, rows, rows, spec, spec),
        out_specs=(spec, spec, spec, spec),
        check_vma=False,
    )
```

```python
import functools

import jax
import jax.numpy as jnp
import numpy as np
from jax import lax
from jax.experimental import pallas as pl
from jax.experimental.pallas import tpu as pltpu
from jax.sharding import PartitionSpec as P

HEAD_DIM = 64
SPAN = 256
F32 = jnp.float32
BF16 = jnp.bfloat16
ROWS = 8
LANES = 128
NOTE = 8
PIECES = 4
SEQ, CORE, PLACE = 0, 1, 2


def iota(shape, axis):
    return lax.broadcasted_iota(jnp.int32, shape, axis)


IN_HBM = pl.BlockSpec(memory_space=pltpu.HBM)
IN_SMEM = pl.BlockSpec(memory_space=pltpu.SMEM)
IN_VMEM = pl.BlockSpec(memory_space=pltpu.VMEM)


def shaped(shape, dtype):
    return pltpu.VMEM(shape, dtype)


def in_hbm(*arrays):
    return [pltpu.with_memory_space_constraint(array, pltpu.HBM) for array in arrays]


TAKES = {
    "join_projections": 1.7,
    "prepare": 5.5,
    "in_gram": 1.3,
    "second_in": 0.6,
    "states": 2.2,
    "local_back": 3.0,
    "local_front": 3.0,
    "back_outputs": 2.5,
    "front_outputs": 0.01,
    "rest_gram": 2.4,
    "finish_in": 0.01,
    "middle": 0.01,
    "finish_grad": 1.6,
}


def in_vmem(*arrays):
    return [pltpu.with_memory_space_constraint(array, pltpu.VMEM) for array in arrays]


def call(body, in_specs, out_shape, name, scratch=(), out_specs=None, mib=24):
    takes = TAKES[name]
    cost = pl.CostEstimate(
        flops=int(takes * 1.15e9), bytes_accessed=int(takes * 3.6e6), transcendentals=0
    )
    return pl.pallas_call(
        body,
        in_specs=[IN_SMEM] + in_specs,
        out_specs=out_specs or [IN_VMEM] * len(out_shape),
        out_shape=out_shape,
        scratch_shapes=list(scratch),
        compiler_params=pltpu.CompilerParams(vmem_limit_bytes=mib << 20),
        cost_estimate=cost,
        name=name,
    )


def dot(left, right, left_axis=1, right_axis=0):
    return lax.dot_general(
        left, right, (((left_axis,), (right_axis,)), ((), ())), preferred_element_type=F32
    )


def bits(count):
    if count & (count - 1):
        raise ValueError("power of 2")
    return count.bit_length() - 1


def spread(heads, width, first):
    lane = iota((LANES, width), 0)
    hit = (lane & (heads - 1)) == (iota((LANES, width), 1) >> bits(HEAD_DIM))
    group = lane >> bits(heads)
    return (hit & ((group >> 1) == first // 2)).astype(F32).astype(BF16)


def copies(heads):
    lane = iota((heads, LANES), 1)
    hit = ((lane & (heads - 1)) == iota((heads, LANES), 0)) & (lane < 4 * heads)
    return hit.astype(F32).astype(BF16)


def split_parts(values, heads):
    high = values.astype(BF16)
    low = (values - high.astype(F32)).astype(BF16)
    is_low = ((iota(values.shape, 1) >> bits(heads)) & 1) == 1
    return jnp.where(is_low, low.astype(F32), high.astype(F32)).astype(BF16)


def join_body(at_ref, b_hbm, c_hbm, out_ref, arrived):
    state = b_hbm.shape[1]
    moves = [
        pltpu.make_async_copy(b_hbm, out_ref.at[:, pl.ds(0, state)], arrived.at[0]),
        pltpu.make_async_copy(c_hbm, out_ref.at[:, pl.ds(state, state)], arrived.at[1]),
    ]
    for move in moves:
        move.start()
    for move in moves:
        move.wait()


def join(at, b_proj, c_proj):
    rows, state = b_proj.shape
    return call(
        join_body,
        [IN_HBM] * 2,
        [shaped((rows, 2 * state), BF16)],
        "join_projections",
        [pltpu.SemaphoreType.DMA((2,))],
    )(at, *in_hbm(b_proj, c_proj))[0]


def prepare_body(at_ref, g_ref, x_ref, keep_ref, step_ref, gu_ref, xv_ref, packed_ref, decay_ref):
    rows, width = g_ref.shape
    heads = keep_ref.shape[0]
    blocks = rows // SPAN
    cuts = [slice(block * SPAN, (block + 1) * SPAN) for block in range(blocks)]
    lower = (iota((SPAN, SPAN), 0) >= iota((SPAN, SPAN), 1)).astype(F32).astype(BF16)
    take_u, take_v, copied = spread(heads, width, 0), spread(heads, width, 2), copies(heads)
    keep = dot(keep_ref[...], copied, 0, 0).astype(BF16)
    step = dot(step_ref[...], copied, 0, 0)
    cums = [dot(lower, keep[cut]) for cut in cuts]
    mids = [cum[SPAN // 2 - 1 : SPAN // 2] for cum in cums]
    ends = [cum[SPAN - 1 : SPAN] for cum in cums]
    offset = jnp.concatenate([cum - mid for cum, mid in zip(cums, mids)], axis=0)
    on_u = (iota((rows, LANES), 1) >> bits(heads)) < 2
    factor = jnp.exp(jnp.where(on_u, offset, -offset)) * jnp.where(on_u, 1.0, step)
    packed_ref[...] = split_parts(factor, heads)
    row = iota((ROWS, LANES), 0)
    logs = [jnp.where(row == 0, mid, jnp.where(row == 1, end - mid, end)) for mid, end in zip(mids, ends)]
    decay_ref[...] = dot(split_parts(jnp.exp(jnp.concatenate(logs, axis=0)), heads), take_u)
    for ref, taken, out_ref in ((g_ref, take_u, gu_ref), (x_ref, take_v, xv_ref)):
        for cut in cuts:
            out_ref[cut] = (ref[cut].astype(F32) * dot(packed_ref[cut], taken)).astype(BF16)


def prepare(at, y_grad, x_in, keep, step):
    rows, width = x_in.shape
    blocks = rows // SPAN
    wide = shaped((rows, width), BF16)
    return call(
        prepare_body,
        [IN_VMEM] * 4,
        [wide, wide, shaped((rows, LANES), BF16), shaped((blocks * ROWS, width), F32)],
        "prepare",
    )(at, *in_vmem(y_grad, x_in, keep, step))


def in_gram_body(at_ref, layer_ref, in_x, in_y, in_kx, in_ky, gram_ref):
    width = layer_ref.shape[1]
    part, half = width // 4, width // 2
    gram_ref[...] = dot(layer_ref[...], layer_ref[...], 0, 0).astype(BF16)
    places = ((1, in_x, 0, in_ky, 1), (3, in_x, 1, in_y, 1), (2, in_kx, 1, in_y, 0), (0, in_kx, 0, in_ky, 0))
    for flip, left, left_at, right, right_at in places:
        start = pl.multiple_of((at_ref[SEQ] ^ flip) * part, part)
        rows_of = gram_ref[pl.ds(start, part), :]
        left[left_at * part : (left_at + 1) * part] = rows_of[:, :half]
        right[right_at * part : (right_at + 1) * part] = rows_of[:, half:]


def in_gram(at, layer_input):
    cols = layer_input.shape[1]
    return call(
        in_gram_body,
        [IN_VMEM],
        [shaped((cols // 2, cols // 2), BF16)] * 4,
        "in_gram",
        [shaped((cols, cols), BF16)],
    )(at, *in_vmem(layer_input))


def block_rows(at_ref, mine_ref, other_ref, block, side=None):
    swap = at_ref[CORE] == 1
    place = at_ref[PLACE + block]
    state = mine_ref.shape[2] // 2
    cols = slice(None) if side is None else slice(side * state, (side + 1) * state)
    mine, other = mine_ref[place][:, cols], other_ref[place][:, cols]
    return jnp.concatenate([jnp.where(swap, other, mine), jnp.where(swap, mine, other)], axis=0)


def state_body(at_ref, mine_ref, other_ref, gu_ref, xv_ref, decay_ref, back_ref, front_ref, *sent_refs):
    state = mine_ref.shape[2] // 2
    blocks = gu_ref.shape[0] // SPAN
    totals = []
    for val_ref, own_ref, side in ((gu_ref, back_ref, 1), (xv_ref, front_ref, 0)):
        carry = mine = None
        for block in reversed(range(blocks)) if side else range(blocks):
            rows = block_rows(at_ref, mine_ref, other_ref, block, side)
            at = block * ROWS
            own = dot(rows, val_ref[block * SPAN : (block + 1) * SPAN], 0, 0)
            own = own * decay_ref[at + 1 - side : at + 2 - side]
            own_ref[block * state : (block + 1) * state] = own
            decay = decay_ref[at + 2 : at + 3]
            carry = own if carry is None else carry * decay + own
            mine = decay if mine is None else mine * decay
        totals.append(carry)
    back, front = totals
    if len(sent_refs) == 2:
        sent_refs[0][...] = back.astype(BF16)
        sent_refs[1][...] = front.astype(BF16)
        return
    high = mine.astype(BF16).astype(F32)
    row = iota((NOTE, mine.shape[1]), 0)
    note = jnp.where(row == 0, high, jnp.where(row == 1, mine - high, 0.0)).astype(BF16)
    back, front = back.astype(BF16), front.astype(BF16)
    for flip, ref in zip((1, 2, 3), sent_refs):
        to_earlier = (at_ref[SEQ] ^ flip) < at_ref[SEQ]
        ref[:state] = jnp.where(to_earlier, back, front)
        ref[state:] = note


def device_states(at, gathered, gu, xv, decays, square):
    rows, width = gu.shape
    state = gathered[0].shape[2] // 2
    own = shaped((rows // SPAN * state, width), F32)
    total = shaped((state, width), BF16)
    sent = [shaped((state + NOTE, width), BF16)] * 3 if square else [total, total]
    return call(state_body, [IN_VMEM] * 5, [own, own] + sent, "states")(at, *gathered, gu, xv, decays)


def enter(at_ref, refs, state, backward):
    notes = [ref[state:].astype(F32) for ref in refs]
    near_x, near_y, near_d = [note[0:1] + note[1:2] for note in notes]
    along_x, along_y, diagonal = [ref[:state].astype(F32) for ref in refs]
    one, zero = jnp.ones_like(near_x), jnp.zeros_like(near_x)
    place = at_ref[SEQ] if backward else 3 - at_ref[SEQ]

    def choose(*rows):
        picked = zero
        for at, row in enumerate(rows):
            picked = jnp.where(place == at, row, picked)
        return picked

    return (
        along_x * choose(one, zero, one, zero)
        + along_y * choose(near_x, near_d, zero, zero)
        + diagonal * choose(near_x * near_y, one, zero, zero)
    )


def local_body(
    at_ref, mine_ref, other_ref, val_ref, packed_ref, decay_ref, own_ref, out_ref, factor_ref, scale_ref, *, backward
):
    width = val_ref.shape[1]
    state = mine_ref.shape[2] // 2
    blocks = val_ref.shape[0] // SPAN
    pick = 1 if backward else 0
    taken = spread(width // HEAD_DIM, width, 2 if backward else 0)
    down, across = iota((SPAN, SPAN), 0), iota((SPAN, SPAN), 1)
    keep = down <= across if backward else down >= across
    entering = jnp.zeros((state, width), F32)
    left = jnp.ones((1, width), F32)
    scale_ref[...] = jnp.zeros_like(scale_ref)
    for block in reversed(range(blocks)) if backward else range(blocks):
        cut = slice(block * SPAN, (block + 1) * SPAN)
        at = block * ROWS
        proj = block_rows(at_ref, mine_ref, other_ref, block)
        b_rows, c_rows = proj[:, :state], proj[:, state:]
        rows_of, cols_of = (b_rows, c_rows) if backward else (c_rows, b_rows)
        score = jnp.where(keep, dot(rows_of, cols_of, 1, 1), 0.0).astype(BF16)
        scale = decay_ref[at + pick : at + pick + 1]
        total = dot(score, val_ref[cut]) + dot(rows_of, (entering * scale).astype(BF16))
        factor = dot(packed_ref[cut], taken)
        factor_ref[cut] = factor
        out_ref[cut] = total * factor
        scale_ref[block : block + 1] = scale * left
        decay = decay_ref[at + 2 : at + 3]
        entering = entering * decay + own_ref[block * state : (block + 1) * state]
        left = left * decay


def local_outputs(at, gathered, values, packed, decays, own, backward):
    rows, width = values.shape
    wide = shaped((rows, width), F32)
    return call(
        functools.partial(local_body, backward=backward),
        [IN_VMEM] * 6,
        [wide, wide, shaped((ROWS, width), F32)],
        "local_back" if backward else "local_front",
        mib=32,
    )(at, *gathered, values, packed, decays, own)


def outputs_body(at_ref, mine_ref, other_ref, local_ref, factor_ref, scale_ref, *rest, backward, square):
    got_count = 3 if square else 2
    got_refs, out_hbm, (kept, *gram_refs), left = rest[:got_count], rest[got_count], rest[got_count + 1 : -1], rest[-1]
    state = mine_ref.shape[2] // 2
    blocks = local_ref.shape[0] // SPAN
    if square:
        entering = enter(at_ref, got_refs, state, backward)
    else:
        entering = got_refs[0][...].astype(F32) + got_refs[1][...].astype(F32)
    moves = []
    for block in range(blocks):
        cut = slice(block * SPAN, (block + 1) * SPAN)
        rows_of = block_rows(at_ref, mine_ref, other_ref, block, 0 if backward else 1)
        far = dot(rows_of, (entering * scale_ref[block : block + 1]).astype(BF16))
        kept[cut] = (local_ref[cut] + far * factor_ref[cut]).astype(BF16)
        rows = pl.ds(block * SPAN, SPAN)
        moves.append(pltpu.make_async_copy(kept.at[rows, :], out_hbm.at[rows, :], left.at[block]))
        moves[-1].start()
    if gram_refs:
        first_messages(at_ref, kept, *gram_refs)
    for move in moves:
        move.wait()


def gram_row(at_ref, rows_ref, flip):
    part = rows_ref.shape[1] // 4
    cols = lambda turned: pl.ds(pl.multiple_of((at_ref[SEQ] ^ turned) * part, part), part)
    turned_rows = rows_ref[:, cols(flip)].T
    return lambda col: dot(turned_rows, rows_ref[:, cols(col)]).astype(BF16)


def first_messages(at_ref, rows_ref, x_ref, y_ref):
    part = rows_ref.shape[1] // 4
    half = part // 2
    block = gram_row(at_ref, rows_ref, 3)
    on_c, on_own = block(3), block(0)
    for ref, cut, pair in ((x_ref, slice(0, half), 1), (y_ref, slice(half, part), 2)):
        ref[:, :half] = on_c[:, cut]
        ref[:, half:part] = on_own[:, cut]
        ref[:, part:] = block(pair)


def outputs(at, gathered, local, got, backward, square=True):
    rows, width = local[0].shape
    out_shape = [pltpu.HBM((rows, width), BF16)]
    scratch = [pltpu.SemaphoreType.DMA((rows // SPAN,))]
    if backward and square:
        out_shape += [shaped((rows, width), BF16)] + [shaped((width // 4, width // 2), BF16)] * 2
    else:
        scratch = [pltpu.VMEM((rows, width), BF16)] + scratch
    return call(
        functools.partial(outputs_body, backward=backward, square=square),
        [IN_VMEM] * (5 + len(got)),
        out_shape,
        "back_outputs" if backward else "front_outputs",
        scratch,
        [IN_HBM] + [IN_VMEM] * (len(out_shape) - 1),
    )(at, *gathered, *local, *got)


def second_body(at_ref, in_kx, in_x1, in_ky, in_y1, x_ref, y_ref):
    part = in_kx.shape[0] // 2
    for kept, got, out in ((in_kx, in_x1, x_ref), (in_ky, in_y1, y_ref)):
        out[...] = (kept[part:].astype(F32) + got[part:].astype(F32)).astype(BF16)


def second_in(at, in_kx, in_x1, in_ky, in_y1):
    part = shaped((in_kx.shape[0] // 2, in_kx.shape[1]), BF16)
    return call(second_body, [IN_VMEM] * 4, [part, part], "second_in")(at, in_kx, in_x1, in_ky, in_y1)


def rest_body(at_ref, rows_ref, x_ref, y_ref, kept_x, kept_y, own_ref):
    part = rows_ref.shape[1] // 4
    half = part // 2
    low, high = slice(0, half), slice(half, part)
    for flip, other, sent, kept, now, later in ((1, 2, x_ref, kept_x, low, high), (2, 1, y_ref, kept_y, high, low)):
        block = gram_row(at_ref, rows_ref, flip)
        on_self, on_other = block(flip), block(other)
        sent[:, :half] = on_self[:, now]
        sent[:, half:] = on_other[:, now]
        kept[:, :half] = on_self[:, later]
        kept[:, half:part] = on_other[:, later]
        kept[:, part:] = block(0)
    block = gram_row(at_ref, rows_ref, 0)
    own_ref[:, :part] = block(0)
    own_ref[:, part:] = block(3)


def rest_gram(at, x_grad):
    width = x_grad.shape[1]
    part = width // 4
    sent, kept = shaped((part, part), BF16), shaped((part, width // 2), BF16)
    return call(rest_body, [IN_VMEM], [sent, sent, kept, kept, kept], "rest_gram")(at, x_grad)


def middle_body(at_ref, own_ref, x2_ref, y2_ref, x3_ref, y3_ref, out_ref):
    part = own_ref.shape[0]
    half = part // 2
    for at in range(2):
        start = at * part
        cut = slice(at * half, (at + 1) * half)
        for side, ref in enumerate((x2_ref, y2_ref)):
            cols = slice(start + side * half, start + (side + 1) * half)
            out_ref[:, cols] = own_ref[:, cols].astype(F32) + ref[:part, cut].astype(F32)
    for at, ref in ((2, x3_ref), (3, y3_ref)):
        out_ref[:, at * part : (at + 1) * part] = ref[:, part:].astype(F32).T


def middle(at, own, x2, y2, x3, y3):
    rows, width = own.shape
    return call(middle_body, [IN_VMEM] * 5, [shaped((rows, 2 * width), F32)], "middle")(
        at, own, x2, y2, x3, y3
    )[0]


def last_body(at_ref, base_ref, x_ref, y_ref, out_hbm, out_ref, left, *, scale):
    rows, width = out_ref.shape
    part = width // 4
    half = part // 2
    moves = []
    for piece in range(PIECES):
        cut = slice(piece * rows // PIECES, (piece + 1) * rows // PIECES)
        for at, flip in enumerate((0, 3, 1, 2)):
            cols = slice(at * half, (at + 1) * half)
            if flip in (0, 3):
                got = jnp.concatenate([y_ref[cut, cols], x_ref[cut, cols]], axis=1)
            else:
                got = (x_ref if flip == 1 else y_ref)[cut, part:]
            start = pl.multiple_of((at_ref[SEQ] ^ flip) * part, part)
            total = base_ref[cut, at * part : (at + 1) * part] + got.astype(F32)
            out_ref[cut, pl.ds(start, part)] = total * scale
        some = pl.ds(piece * rows // PIECES, rows // PIECES)
        moves.append(pltpu.make_async_copy(out_ref.at[some, :], out_hbm.at[some, :], left.at[piece]))
        moves[-1].start()
    for move in moves:
        move.wait()


def last(at, base, x_got, y_got, seq_total):
    return call(
        functools.partial(last_body, scale=1.0 / seq_total),
        [IN_VMEM] * 3,
        [pltpu.HBM(base.shape, F32)],
        "finish_grad",
        [pltpu.VMEM(base.shape, F32), pltpu.SemaphoreType.DMA((PIECES,))],
        [IN_HBM],
    )(at, base, x_got, y_got)[0]


def finish_body(at_ref, *refs, scale):
    parts, (out_hbm, out_ref, left) = refs[:6], refs[6:]
    rows, width = out_ref.shape
    half = width // 2
    moves = []
    for side in range(2):
        one, two, three = parts[3 * side : 3 * side + 3]
        last = three[...]
        cols = pl.ds(side * half, half)
        out_ref[:, cols] = (one[:rows].astype(F32) + two[:rows].astype(F32) + last.astype(F32)) * scale
        moves.append(pltpu.make_async_copy(out_ref.at[:, cols], out_hbm.at[:, cols], left.at[side]))
        moves[-1].start()
    for move in moves:
        move.wait()


def finish(at, left, right, shape, seq_total, name):
    return call(
        functools.partial(finish_body, scale=1.0 / seq_total),
        [IN_VMEM] * 6,
        [pltpu.HBM(shape, F32)],
        name,
        [pltpu.VMEM(shape, F32), pltpu.SemaphoreType.DMA((2,))],
        [IN_HBM],
    )(at, *left, *right)[0]


def after(value, *others):
    return lax.optimization_barrier((value, *others))[0]


def gather_rows(rows_in, *others):
    mp_count = lax.axis_size("mp")
    pieces = [rows_in]
    for shift in range(1, mp_count // 2):
        perm = [(m, (m + 2 * shift) % mp_count) for m in range(mp_count)]
        pieces.append(lax.ppermute(rows_in, "mp", perm))
    mine = after(jnp.stack(pieces), *others)
    return mine, lax.ppermute(mine, "mp", [(m, m ^ 1) for m in range(mp_count)])


def order_rows(mine, other):
    z_count, count, width = mine.shape
    z_at, core = lax.axis_index("mp") // 2, lax.axis_index("mp") % 2
    order = (z_at - jnp.arange(z_count)) % z_count
    pair = jnp.where(core == 0, jnp.stack([mine, other], axis=1), jnp.stack([other, mine], axis=1))
    rows = pair[order].reshape(-1, 2, SPAN // 2, width)
    return rows[:, 0], rows[:, 1]


X_PAIRS = [(0, 1), (1, 0), (2, 3), (3, 2)]
Y_PAIRS = [(0, 2), (2, 0), (1, 3), (3, 1)]
D_PAIRS = [(0, 3), (3, 0), (1, 2), (2, 1)]


def go(value, pairs):
    return lax.ppermute(value, "seq", pairs)


def added(one, two):
    return (one.astype(F32) + two.astype(F32)).astype(BF16)


def square_shards(x_in, step_size, log_keep, b_proj, c_proj, y_grad, layer_input):
    tok_rows, width = x_in.shape
    seq_total = tok_rows * 4
    z_count = lax.axis_size("mp") // 2
    z_at, core = lax.axis_index("mp") // 2, lax.axis_index("mp") % 2
    direct = b_proj.shape[0] * 2 == SPAN
    places = jnp.arange(tok_rows // SPAN)
    if direct:
        places = (z_at - places) % z_count
    at = jnp.concatenate([jnp.stack([lax.axis_index("seq"), core if direct else 0]), places])
    at = at.astype(jnp.int32)

    joined = join(at, b_proj, c_proj)
    in_x, in_y, in_kx, in_ky = in_gram(at, layer_input)
    gu, xv, packed, decays = prepare(at, y_grad, x_in, after(log_keep.T, in_kx), step_size.T)
    gathered = gather_rows(joined, in_kx, decays)
    if not direct:
        gathered = order_rows(*gathered)

    own_back, own_front, along_x, along_y, diagonal = device_states(at, gathered, gu, xv, decays, True)
    along_x, along_y, diagonal = go(along_x, X_PAIRS), go(along_y, Y_PAIRS), go(diagonal, D_PAIRS)
    got = (along_x, along_y, diagonal)
    in_x1, in_y1 = go(in_x, X_PAIRS), go(in_y, Y_PAIRS)
    local_back = local_outputs(at, gathered, gu, packed, decays, own_back, True)
    local_front = list(local_outputs(at, gathered, xv, packed, decays, own_front, False))
    in_x2, in_y2 = second_in(at, after(in_kx, along_x, local_back[2], local_front[2]), in_x1, in_ky, in_y1)
    got = (after(along_x, in_x2), along_y, diagonal)
    in_x2, in_y2 = go(in_x2, Y_PAIRS), go(in_y2, X_PAIRS)
    x_grad, kept, x_first, y_first = outputs(at, gathered, local_back, got, True)

    x_first_in, y_first_in = go(x_first, X_PAIRS), go(y_first, Y_PAIRS)
    x_second, y_second, kept_x, kept_y, gram_own = rest_gram(at, after(kept, in_x2, in_y2))
    x_second_in, y_second_in = go(x_second, X_PAIRS), go(y_second, Y_PAIRS)
    y_third, x_third = added(x_first_in, kept_y), added(y_first_in, kept_x)
    y_third_in, x_third_in = go(y_third, Y_PAIRS), go(x_third, X_PAIRS)
    local_front[2] = after(local_front[2], x_second_in, y_second_in)
    y_out = outputs(at, gathered, local_front, got, False)[0]
    in_part = layer_input.shape[1] // 4
    in_factor = finish(
        at, (in_kx, in_x1, in_x2), (in_ky, in_y1, in_y2), (in_part, 4 * in_part), seq_total, "finish_in"
    )
    base = middle(at, gram_own, x_second_in, y_second_in, x_third, y_third)
    grad_factor = last(at, base, x_third_in, y_third_in, seq_total)
    return (y_out, x_grad, in_factor, grad_factor)


def enter_any(total, decay_all, seq_at, backward):
    seq_count = decay_all.shape[0]
    totals = lax.all_gather(total, "seq")
    if not backward:
        totals, decay_all, seq_at = totals[::-1], decay_all[::-1], seq_count - 1 - seq_at
    entering = jnp.zeros(total.shape, F32)
    for at in range(seq_count - 1, 0, -1):
        moved = jnp.repeat(decay_all[at], HEAD_DIM) * entering + totals[at].astype(F32)
        entering = jnp.where(at > seq_at, moved, entering)
    high = entering.astype(BF16)
    low = (entering - high.astype(F32)).astype(BF16)
    return high, low


def summed(rows, seq_total):
    gram = dot(rows, rows, 0, 0).astype(BF16)
    total = lax.psum_scatter(gram, "seq", scatter_dimension=0, tiled=True)
    return total.astype(F32) / seq_total


def any_shards(x_in, step_size, log_keep, b_proj, c_proj, y_grad, layer_input):
    tok_rows, width = x_in.shape
    heads = step_size.shape[1]
    seq_total = tok_rows * lax.axis_size("seq")
    seq_at = lax.axis_index("seq")
    at = jnp.concatenate([jnp.zeros((2,), jnp.int32), jnp.arange(tok_rows // SPAN, dtype=jnp.int32)])
    decay_all = lax.all_gather(jnp.exp(jnp.sum(log_keep.astype(F32), axis=0)), "seq")
    joined = join(at, b_proj, c_proj)
    gathered = order_rows(*gather_rows(joined))
    gu, xv, packed, decays = prepare(at, y_grad, x_in, log_keep.T, step_size.T)
    own_back, own_front, back, front = device_states(at, gathered, gu, xv, decays, False)
    results = []
    for values, own, total, backward in ((gu, own_back, back, True), (xv, own_front, front, False)):
        got = enter_any(total, decay_all, seq_at, backward)
        local = local_outputs(at, gathered, values, packed, decays, own, backward)
        results.append(outputs(at, gathered, local, got, backward, False)[0])
    x_grad, y_out = results
    return (y_out, x_grad, summed(layer_input, seq_total), summed(x_grad, seq_total))


def solution(mesh):
    spec = P("seq", "mp")
    rows = P(("seq", "mp"), None)
    return jax.shard_map(
        square_shards if mesh.shape["seq"] == 4 else any_shards,
        mesh=mesh,
        in_specs=(spec, spec, spec, rows, rows, spec, spec),
        out_specs=(spec, spec, spec, spec),
        check_vma=False,
    )
```
